32 devices in a mesh: seq: 8 (over z, y), blk: 2 (over x), clip: 2 (over core).
Axes of the slice: x: 2, y: 2, z: 4, core: 2. Of those that a mesh axis runs over, the one named last changes fastest.
Arguments:
- modulated: bfloat16 [24576, 3072], P(('clip', 'seq', 'blk')), parts along dimension 0, may hold values from -16 to 16
- mod_gate: float32 [6144], P('clip'), parts along dimension 0, may hold values from 0.5 to 1.5
- w_qkv: bfloat16 [3072, 4608], P(None, 'blk'), may hold values from -0.109375 to 0.109375
- w_out: bfloat16 [1536, 3072], P(None, 'blk'), may hold values from -0.15625 to 0.15625
- kv_tiles: int32 [64, 6], P('clip'), parts along dimension 0, may hold values from 0 to 31, as said below
- kv_count: int32 [64], P('clip'), parts along dimension 0, may hold values from 1 to 6, as said below
Outputs:
- update: bfloat16 [24576, 3072], P(('clip', 'seq', 'blk')), parts along dimension 0
The draws below stay inside these ranges and needn't reach their ends.
There are 2 independent parts, one for each index of `clip`. The reference program is written for one: setup_inputs(seed, part) draws one part's arguments, and reference() takes and returns one part's arrays. A program takes and returns all parts, laid end to end along the dimension named above; an argument that names none is the same for every part. Nothing has to cross between parts.
Inputs may be any that keep to these rules, and one draw needn't show every extreme that they name: Row i of kv_tiles lists 6 different tiles; each of their three tile coordinates differs from tile i's by at most one. `kv_count`: some tile uses all 6 listed tiles.
All inputs are finite; a program needn't handle non-finite values.
Results may differ from the reference program's by a relative error of at most 0.011.
Values may be sent and summed in bfloat16 or wider, within the bound.
No kernel may reach another device: no remote copies, remote signals or barrier semaphores. Data moves between devices by JAX's collectives and lax.ppermute only.
A program may use at most 192 MiB of HBM per device.

```python
import jax
import jax.numpy as jnp
from jax import lax

D = 3072
HD = 128
NH = 12
TF = 6
TH = 8
TW = 8
NB = 6
GH = 2
GF = 2
NTILES = 32
TOKENS = 12288
N_SEQ = 8


def draw_modulated(key, part):
    first = jax.random.fold_in(key, 0)
    values = jnp.clip(jax.random.normal(first, (TOKENS, D), jnp.float32), -6.0, 6.0)
    return values.astype(jnp.bfloat16)


def draw_kv_tiles(key, part):
    key = jax.random.fold_in(key, 11)
    tile_ids = jnp.arange(NTILES, dtype=jnp.int32)
    tile_col = tile_ids % N_SEQ
    layer_row = tile_ids // N_SEQ
    tile_row = layer_row % GH
    tile_layer = layer_row // GH
    offsets = jnp.arange(27, dtype=jnp.int32)
    off_layer = offsets // 9 - 1
    off_row = offsets // 3 % 3 - 1
    off_col = offsets % 3 - 1
    near_layer = tile_layer[:, None] + off_layer[None, :]
    near_row = tile_row[:, None] + off_row[None, :]
    near_col = tile_col[:, None] + off_col[None, :]
    inside = (near_layer >= 0) & (near_layer < GF) & (near_row >= 0) & (near_row < GH)
    inside = inside & (near_col >= 0) & (near_col < N_SEQ)
    ranks = jax.random.randint(key, (NTILES, 27), 0, 4096, dtype=jnp.int32) * 32 + offsets[None, :]
    ranks = jnp.where(inside, ranks, offsets[None, :] - 100)
    unused, chosen = lax.top_k(ranks, NB)
    near_ids = (near_layer * GH + near_row) * N_SEQ + near_col
    return jnp.take_along_axis(near_ids, chosen, axis=1).astype(jnp.int32)


def draw_kv_count(key, part):
    key = jax.random.fold_in(key, 23)
    first, second = jax.random.split(key, 2)
    counts = jax.random.randint(first, (NTILES,), 1, NB + 1, dtype=jnp.int32)
    spot = jax.random.randint(second, (), 0, NTILES, dtype=jnp.int32)
    counts = counts.at[spot].set(NB)
    return counts.astype(jnp.int32)


def steps_of(rng, extent, cuts, smallest, top_value):
    gain = 1.0
    for dim, blocks in cuts:
        steps = jax.random.uniform(jax.random.fold_in(jax.random.fold_in(rng, 6), dim), (blocks,), jnp.float32, smallest / len(cuts), top_value / len(cuts))
        gain = gain * jnp.repeat(jnp.exp(steps), extent[dim] // blocks).reshape((-1,) + (1,) * (len(extent) - 1 - dim))
    return gain


def normal_values(rng, extent, spread, bound, cuts=(), kind=jnp.bfloat16):
    drawn = spread * jax.random.normal(rng, extent, jnp.float32)
    if cuts:
        drawn = drawn * steps_of(rng, extent, cuts, -0.22, 0.18)
    return jnp.clip(drawn, -bound, bound).astype(kind)


def setup_inputs(seed: int = 0, part: int = 0) -> dict:
    key_of = jax.random.split(jax.random.key(seed), 7)
    part_splits = jax.random.split(jax.random.fold_in(key_of[6], part), 7)
    modulated = draw_modulated(jax.random.fold_in(jax.random.fold_in(key_of[6], part), 71), part)
    mod_gate = jnp.clip(jax.random.uniform(part_splits[1], (D,), jnp.float32, 0.5, 1.5), 0.5, 1.5)
    w_qkv = normal_values(key_of[2], (D, NH * 3 * HD), D ** -0.5, 0.109375, ((1, 2),))
    w_out = normal_values(key_of[3], (NH * HD, D), (NH * HD) ** -0.5, 0.15625, ((1, 2),))
    kv_tiles = draw_kv_tiles(jax.random.fold_in(jax.random.fold_in(key_of[6], part), 71), part)
    kv_count = draw_kv_count(jax.random.fold_in(jax.random.fold_in(key_of[6], part), 71), part)
    return dict(modulated=modulated, mod_gate=mod_gate, w_qkv=w_qkv, w_out=w_out, kv_tiles=kv_tiles, kv_count=kv_count)


def reference(modulated, mod_gate, w_qkv, w_out, kv_tiles, kv_count):
    projected = jnp.dot(modulated, w_qkv, preferred_element_type=jnp.float32).astype(jnp.bfloat16)
    tile_cells = TF * TH * TW
    tiled = projected.reshape(GF, TF, GH, TH, N_SEQ, TW, NH, 3, HD)
    tiled = tiled.transpose(0, 2, 4, 1, 3, 5, 6, 7, 8).reshape(NTILES, tile_cells, NH, 3, HD)
    queries = tiled[:, :, :, 0]
    keys_all = tiled[:, :, :, 1]
    values_all = tiled[:, :, :, 2]
    score_scale = 1.0 / (HD ** 0.5)

    def one_tile(index):
        query = queries[index].astype(jnp.float32)
        listed = kv_tiles[index]
        picked_keys = jnp.take(keys_all, listed, axis=0).astype(jnp.float32)
        picked_values = jnp.take(values_all, listed, axis=0).astype(jnp.float32)
        scores = jnp.einsum("tnd,jsnd->ntjs", query, picked_keys) * score_scale
        open_slot = jnp.arange(NB, dtype=jnp.int32) < kv_count[index]
        scores = jnp.where(open_slot[None, None, :, None], scores, -jnp.inf)
        peak_score = jnp.max(scores, axis=(2, 3), keepdims=True)
        weights = jnp.exp(scores - peak_score)
        denom_sum = jnp.sum(weights, axis=(2, 3))
        rounded = lax.optimization_barrier(weights.astype(jnp.bfloat16)).astype(jnp.float32)
        mixed = jnp.einsum("ntjs,jsnd->tnd", rounded, picked_values)
        mixed = mixed / jnp.transpose(denom_sum)[:, :, None]
        return mixed.astype(jnp.bfloat16)

    attended = lax.map(one_tile, jnp.arange(NTILES, dtype=jnp.int32))
    ordered = attended.reshape(GF, GH, N_SEQ, TF, TH, TW, NH, HD)
    ordered = ordered.transpose(0, 3, 1, 4, 2, 5, 6, 7).reshape(TOKENS, NH * HD)
    product = jnp.dot(ordered, w_out, preferred_element_type=jnp.float32)
    return (product * mod_gate).astype(jnp.bfloat16)
```

```python
import functools
import math

import jax
import jax.numpy as jnp
from jax import lax
from jax.experimental import pallas as pl
from jax.experimental.pallas import tpu as pltpu
from jax.sharding import PartitionSpec as P

HD = 128
NH = 12
TF = 6
TH = 8
TW = 8
NB = 6
GH = 2
CELLS = TF * TH * TW
AXES = ("seq", "blk", "clip")
GROUPS = 4
HPD = NH // GROUPS
EXP2_SCALE = math.log2(math.e) / math.sqrt(HD)
MIB = 1 << 20


def permuted(array, seq_count, target):
    pairs = []
    for seq in range(seq_count):
        for blk in range(2):
            for clip in range(2):
                goal = target(seq // 2, seq % 2, blk, clip)
                if goal is not None:
                    strip, half, blk_to, clip_to = goal
                    pairs.append(
                        ((seq * 2 + blk) * 2 + clip, ((strip * 2 + half) * 2 + blk_to) * 2 + clip_to)
                    )
    return lax.ppermute(array, AXES, pairs)


def projection_body(first, place, *refs):
    pieces, weight = refs[:4], refs[4]
    skip = 5 if first else 5 + 3 * HPD
    outs = refs[skip : skip + 3 * HPD]
    tokens, columns, blocks, token_sem, weight_sem, out_sem = refs[skip + 3 * HPD :]
    piece_rows = pieces[0].shape[0]
    part = piece_rows // 2
    rows = 4 * piece_rows
    loads = []
    for i in range(4):
        start = pl.multiple_of(place[i] * piece_rows, piece_rows)
        loads.append(
            pltpu.make_async_copy(
                pieces[i], tokens.at[pl.ds(start, piece_rows)], token_sem.at[i]
            )
        )
    width = 3 * HD
    streams = []
    for head in range(HPD):
        start = pl.multiple_of((place[5] * HPD + head) * width, HD)
        streams.append(
            pltpu.make_async_copy(
                weight.at[:, pl.ds(start, width)], columns.at[head], weight_sem.at[head]
            )
        )
    for copy in loads:
        copy.start()
    for copy in streams:
        copy.start()
    for copy in loads:
        copy.wait()
    row_start = pl.multiple_of(place[4] * (4 * part), 4 * part)
    stores = []
    for head in range(HPD):
        streams[head].wait()
        total = jnp.dot(tokens[...], columns[head], preferred_element_type=jnp.float32)
        for kind in range(3):
            for column in range(2):
                block = jnp.concatenate(
                    [
                        total[
                            i * piece_rows + column * part : i * piece_rows + (column + 1) * part,
                            kind * HD : (kind + 1) * HD,
                        ]
                        for i in range(4)
                    ],
                    axis=0,
                )
                blocks[head, kind, column] = block.astype(jnp.bfloat16)
                if kind == 0:
                    target = outs[head * 3].at[column, pl.ds(row_start, 4 * part)]
                else:
                    target = outs[head * 3 + 1 + column].at[kind - 1, pl.ds(row_start, 4 * part)]
                copy = pltpu.make_async_copy(
                    blocks.at[head, kind, column],
                    target,
                    out_sem.at[(head * 3 + kind) * 2 + column],
                )
                copy.start()
                stores.append(copy)
    for copy in stores:
        copy.wait()


def project(place, pieces, weight, before, strip_tokens):
    piece_rows, depth = pieces[0].shape
    first = before is None
    out_shape = [jax.ShapeDtypeStruct((2, strip_tokens, HD), jnp.bfloat16)] * (3 * HPD)
    operands = list(pieces) + [weight] + ([] if first else list(before))
    anywhere = pl.BlockSpec(memory_space=pl.ANY)
    return pl.pallas_call(
        functools.partial(projection_body, first),
        out_shape=out_shape,
        in_specs=[pl.BlockSpec(memory_space=pltpu.SMEM)] + [anywhere] * len(operands),
        out_specs=[anywhere] * len(out_shape),
        scratch_shapes=[
            pltpu.VMEM((4 * piece_rows, depth), jnp.bfloat16),
            pltpu.VMEM((HPD, depth, 3 * HD), jnp.bfloat16),
            pltpu.VMEM((HPD, 3, 2, 2 * piece_rows, HD), jnp.bfloat16),
            pltpu.SemaphoreType.DMA((4,)),
            pltpu.SemaphoreType.DMA((HPD,)),
            pltpu.SemaphoreType.DMA((6 * HPD,)),
        ],
        input_output_aliases={} if first else {6 + i: i for i in range(3 * HPD)},
        compiler_params=pltpu.CompilerParams(vmem_limit_bytes=40 * MIB),
        cost_estimate=pl.CostEstimate(
            flops=8 * piece_rows * depth * 3 * HD * HPD,
            bytes_accessed=2 * depth * (4 * piece_rows + 3 * HD * HPD),
            transcendentals=0,
        ),
    )(place, *operands)


def attention_body(
    layers, slots, counts, query, left, own0, own1, right, out, keyvals, scores, peak, denom, mixed, sems
):
    copies = []
    for i, source in enumerate((left, own0, own1, right)):
        copy = pltpu.make_async_copy(source, keyvals.at[i], sems.at[i])
        copy.start()
        copies.append(copy)
    for copy in copies:
        copy.wait()

    def one_tile(tile, carry):
        column = tile // (layers * GH)
        layer = tile // GH % layers
        half = tile % GH
        count = counts[tile]
        queries = query[column, layer, :, half].reshape(CELLS, HD)
        peak[...] = jnp.full(peak.shape, -jnp.inf, jnp.float32)
        denom[...] = jnp.zeros(denom.shape, jnp.float32)
        mixed[...] = jnp.zeros(mixed.shape, jnp.float32)

        def score(slot, inner):
            spot = slots[tile * NB + slot]
            keys = keyvals[spot // (layers * GH), 0, spot // GH % layers, :, spot % GH]
            found = lax.dot_general(
                queries,
                keys.reshape(CELLS, HD),
                (((1,), (1,)), ((), ())),
                preferred_element_type=jnp.float32,
            )
            scores[slot] = found
            top = peak[...]
            for lane in range(CELLS // HD):
                top = jnp.maximum(top, found[:, lane * HD : (lane + 1) * HD])
            peak[...] = top
            return inner

        lax.fori_loop(0, count, score, 0)
        offset = jnp.max(peak[...], axis=1, keepdims=True) * EXP2_SCALE

        def mix(slot, inner):
            spot = slots[tile * NB + slot]
            values = keyvals[spot // (layers * GH), 1, spot // GH % layers, :, spot % GH]
            weights = jnp.exp2(scores[slot] * EXP2_SCALE - offset)
            total = denom[...]
            for lane in range(CELLS // HD):
                total = total + weights[:, lane * HD : (lane + 1) * HD]
            denom[...] = total
            mixed[...] += jnp.dot(
                weights.astype(jnp.bfloat16),
                values.reshape(CELLS, HD),
                preferred_element_type=jnp.float32,
            )
            return inner

        lax.fori_loop(0, count, mix, 0)
        result = mixed[...] / jnp.sum(denom[...], axis=1, keepdims=True)
        out[column, layer, :, half] = result.astype(jnp.bfloat16).reshape(TF, TH * TW, HD)
        return carry

    lax.fori_loop(0, 2 * layers * GH, one_tile, 0)


def attend(slots, counts, query, left, own0, own1, right):
    layers = query.shape[1] // (TF * GH * TH * TW)
    shape = (2, layers, TF, GH, TH * TW, HD)
    smem = pl.BlockSpec(memory_space=pltpu.SMEM)
    vmem = pl.BlockSpec(memory_space=pltpu.VMEM)
    anywhere = pl.BlockSpec(memory_space=pl.ANY)
    out = pl.pallas_call(
        functools.partial(attention_body, layers),
        out_shape=jax.ShapeDtypeStruct(shape, jnp.bfloat16),
        in_specs=[smem, smem, vmem] + [anywhere] * 4,
        out_specs=vmem,
        scratch_shapes=[
            pltpu.VMEM((4,) + shape, jnp.bfloat16),
            pltpu.VMEM((NB, CELLS, CELLS), jnp.float32),
            pltpu.VMEM((CELLS, HD), jnp.float32),
            pltpu.VMEM((CELLS, HD), jnp.float32),
            pltpu.VMEM((CELLS, HD), jnp.float32),
            pltpu.SemaphoreType.DMA((4,)),
        ],
        compiler_params=pltpu.CompilerParams(vmem_limit_bytes=40 * MIB),
        cost_estimate=pl.CostEstimate(
            flops=2 * layers * GH * NB * CELLS * CELLS * HD * 2,
            bytes_accessed=12 * layers * GH * CELLS * HD * 2,
            transcendentals=2 * layers * GH * NB * CELLS * CELLS // 2,
        ),
    )(slots, counts, *[a.reshape(shape) for a in (query, left, own0, own1, right)])
    return out.reshape(query.shape)


def output_body(rounds, rows, strips, *refs):
    pieces = refs[: rounds * HPD]
    weight, gate, out, mixed, sems = refs[rounds * HPD :]
    part = rows * TW

    @pl.when(pl.program_id(0) == 0)
    def _():
        copies = []
        for i in range(rounds):
            for head in range(HPD):
                for group in range(GROUPS):
                    copy = pltpu.make_async_copy(
                        pieces[i * HPD + head].at[group],
                        mixed.at[
                            pl.ds(i * 2 * part, 2 * part),
                            pl.ds((head * GROUPS + group) * HD, HD),
                        ],
                        sems.at[i],
                    )
                    copy.start()
                    copies.append(copy)
        for copy in copies:
            copy.wait()

    product = (
        jnp.dot(mixed[...], weight[...], preferred_element_type=jnp.float32) * gate[...]
    )
    for i in range(rounds):
        strip = strips[i]
        for row in range(rows):
            base = i * 2 * part + row * TW
            both = jnp.concatenate(
                [product[base : base + TW], product[base + part : base + part + TW]], axis=0
            )
            out[row, strip] = both.astype(jnp.bfloat16)


def project_out(strips, pieces, weight, gate, rows):
    rounds = len(pieces) // HPD
    depth, width = weight.shape
    step = 512
    anywhere = pl.BlockSpec(memory_space=pl.ANY)
    return pl.pallas_call(
        lambda strips_ref, *refs: output_body(rounds, rows, strips_ref, *refs),
        out_shape=jax.ShapeDtypeStruct((rows, rounds, 2 * TW, width), jnp.bfloat16),
        grid=(width // step,),
        in_specs=[pl.BlockSpec(memory_space=pltpu.SMEM)]
        + [anywhere] * len(pieces)
        + [
            pl.BlockSpec((depth, step), lambda n: (0, n)),
            pl.BlockSpec((1, step), lambda n: (0, n)),
        ],
        out_specs=pl.BlockSpec((rows, rounds, 2 * TW, step), lambda n: (0, 0, 0, n)),
        scratch_shapes=[
            pltpu.VMEM((rounds * rows * 2 * TW, depth), jnp.bfloat16),
            pltpu.SemaphoreType.DMA((rounds,)),
        ],
        compiler_params=pltpu.CompilerParams(vmem_limit_bytes=40 * MIB),
    )(strips, *pieces, weight, gate)


def local(modulated, mod_gate, w_qkv, w_out, kv_tiles, kv_count):
    tok_rows, depth = modulated.shape
    seq_count = lax.axis_size("seq")
    rounds = seq_count // 2
    rows = tok_rows // (seq_count * TW)
    part = rows * TW
    strip_tokens = rounds * 4 * part
    layers = strip_tokens // (TF * GH * TH * TW)
    seq_index = lax.axis_index("seq")
    strip, half = seq_index // 2, seq_index % 2
    blk, clip = lax.axis_index("blk"), lax.axis_index("clip")

    def swap(array, over_blk, over_clip):
        return permuted(
            array, seq_count, lambda s, h, b, c: (s, h, b ^ over_blk, c ^ over_clip)
        )

    def regroup(array, distance):
        return permuted(array, seq_count, lambda s, h, b, c: (s ^ distance, c, b, h))

    by_strip = modulated.reshape(rows, rounds, 2, TW, depth)
    pieces = []
    for i in range(rounds):
        sent = lax.dynamic_index_in_dim(by_strip, strip ^ i, 1, keepdims=False)
        sent = sent.transpose(1, 0, 2, 3).reshape(2 * part, depth)
        pieces.append(regroup(sent, i))
    quads = []
    for piece in pieces:
        across = swap(piece, 1, 0)
        quads.append((piece, across, swap(piece, 0, 1), swap(across, 0, 1)))

    lists = jnp.concatenate([kv_tiles, kv_count[:, None]], axis=1)
    lists = regroup(lists, 0).reshape(layers * GH, seq_count, NB + 1)
    lists = lax.dynamic_slice_in_dim(lists, strip * 2, 2, axis=1).transpose(1, 0, 2)
    lists = lists.reshape(2 * layers * GH, NB + 1)
    counts = lists[:, NB]
    tiles = lists[:, :NB]
    slots = (tiles % seq_count - strip * 2 + 1) * (layers * GH) + tiles // seq_count
    slots = slots.reshape(-1)

    placed = None
    for i, quad in enumerate(quads):
        place = jnp.stack(
            [
                clip * 2 + blk,
                clip * 2 + 1 - blk,
                (1 - clip) * 2 + blk,
                (1 - clip) * 2 + 1 - blk,
                strip ^ i,
                clip,
            ]
        ).astype(jnp.int32)
        placed = project(place, quad, w_qkv, placed, strip_tokens)

    w_half = w_out.shape[0] // 2
    w_sent = lax.dynamic_slice_in_dim(w_out, clip * w_half, w_half, axis=0)
    w_sent, _ = lax.optimization_barrier((w_sent, quads[-1][1]))
    w_got = swap(w_sent, 1, 0)
    w_also = swap(w_got, 0, 1)
    w_other = jnp.where(
        clip == 0,
        jnp.concatenate([w_got, w_also], axis=0),
        jnp.concatenate([w_also, w_got], axis=0),
    )
    w_full = jnp.where(
        blk == 0,
        jnp.concatenate([w_out, w_other], axis=1),
        jnp.concatenate([w_other, w_out], axis=1),
    )
    w_full = w_full.reshape(2, 2, HPD, HD, -1)
    heads = []
    for head in range(HPD):
        for over_blk, over_clip in ((0, 0), (0, 1), (1, 0), (1, 1)):
            block = lax.dynamic_index_in_dim(w_full, blk ^ over_blk, 0, keepdims=False)
            heads.append(lax.dynamic_index_in_dim(block, half ^ over_clip, 0, keepdims=False)[head])
    w_rows = jnp.concatenate(heads, axis=0)

    returned = [[None] * HPD for _ in range(rounds)]
    for head in range(HPD):
        query, own0, own1 = placed[head * 3 : head * 3 + 3]
        left = permuted(
            own1, seq_count, lambda s, h, b, c: (s + 1, h, b, c) if s + 1 < rounds else None
        )
        right = permuted(own0, seq_count, lambda s, h, b, c: (s - 1, h, b, c) if s else None)
        result = attend(slots, counts, query, left, own0, own1, right)
        result = result.reshape(2, rounds, 2, 2, part, HD)

        def towards(over_blk, over_clip):
            some = lax.dynamic_index_in_dim(result, clip ^ over_clip, 2, keepdims=False)
            return lax.dynamic_index_in_dim(some, blk ^ over_blk, 2, keepdims=False)

        group = jnp.stack(
            [
                towards(0, 0),
                swap(towards(0, 1), 0, 1),
                swap(towards(1, 0), 1, 0),
                swap(towards(1, 1), 1, 1),
            ]
        )
        for i in range(rounds):
            sent = lax.dynamic_index_in_dim(group, strip ^ i, 2, keepdims=False)
            returned[i][head] = regroup(sent.reshape(GROUPS, 2 * part, HD), i)

    strips = jnp.stack([strip ^ i for i in range(rounds)]).astype(jnp.int32)
    flat = [returned[i][head] for i in range(rounds) for head in range(HPD)]
    out = project_out(strips, flat, w_rows, mod_gate.reshape(1, -1), rows)
    return out.reshape(tok_rows, -1)


def solution(mesh):
    return jax.shard_map(
        local,
        mesh=mesh,
        in_specs=(
            P(("clip", "seq", "blk"), None),
            P("clip"),
            P(None, "blk"),
            P(None, "blk"),
            P("clip", None),
            P("clip"),
        ),
        out_specs=P(("clip", "seq", "blk"), None),
        check_vma=False,
    )
```

```python
import functools
import math

import jax
import jax.numpy as jnp
from jax import lax
from jax.experimental import pallas as pl
from jax.experimental.pallas import tpu as pltpu
from jax.sharding import PartitionSpec as P

HD = 128
NH = 12
TF = 6
TH = 8
TW = 8
NB = 6
GH = 2
CELLS = TF * TH * TW
AXES = ("seq", "blk", "clip")
HPD = NH // 2
BATCH = 2
EXP2_SCALE = math.log2(math.e) / math.sqrt(HD)
MIB = 1 << 20
ROW_BLOCK = 192
AHEAD = 1


def permuted(array, seq_count, target):
    pairs = []
    for seq in range(seq_count):
        for blk in range(2):
            for clip in range(2):
                goal = target(seq // 2, seq % 2, blk, clip)
                if goal is not None:
                    strip, half, blk_to, clip_to = goal
                    pairs.append(
                        ((seq * 2 + blk) * 2 + clip, ((strip * 2 + half) * 2 + blk_to) * 2 + clip_to)
                    )
    return lax.ppermute(array, AXES, pairs)


def after(array, *others):
    return lax.optimization_barrier((array,) + others)[0]


def projection_body(count, place, *refs):
    pieces, weight, query, keyval = refs[:count], *refs[count : count + 3]
    tokens, columns, blocks, token_sem, weight_sem, out_sem = refs[count + 3 :]
    piece_rows = pieces[0].shape[0]
    loads = []
    for i in range(count):
        start = pl.multiple_of(place[i] * piece_rows, piece_rows)
        loads.append(
            pltpu.make_async_copy(
                pieces[i], tokens.at[pl.ds(start, piece_rows)], token_sem.at[i]
            )
        )
    width = BATCH * 3 * HD
    streams = []
    for batch in range(HPD // BATCH):
        streams.append(
            pltpu.make_async_copy(
                weight.at[:, pl.ds(batch * width, width)], columns.at[batch], weight_sem.at[batch]
            )
        )
    for copy in loads:
        copy.start()
    for copy in streams:
        copy.start()
    for copy in loads:
        copy.wait()
    stores = []
    for batch in range(HPD // BATCH):
        streams[batch].wait()
        total = jnp.dot(tokens[...], columns[batch], preferred_element_type=jnp.float32)
        for spot in range(BATCH):
            head = batch * BATCH + spot
            for kind in range(3):
                start = (spot * 3 + kind) * HD
                blocks[head, kind] = total[:, start : start + HD].astype(jnp.bfloat16)
            for target, some in (
                (query.at[head], blocks.at[head, 0]),
                (keyval.at[head], blocks.at[head, pl.ds(1, 2)]),
            ):
                copy = pltpu.make_async_copy(some, target, out_sem.at[len(stores)])
                copy.start()
                stores.append(copy)
    for copy in stores:
        copy.wait()


def project(place, pieces, weight):
    count = len(pieces)
    piece_rows, depth = pieces[0].shape
    chunk = count * piece_rows
    anywhere = pl.BlockSpec(memory_space=pl.ANY)
    return pl.pallas_call(
        functools.partial(projection_body, count),
        out_shape=[
            jax.ShapeDtypeStruct((HPD, chunk, HD), jnp.bfloat16),
            jax.ShapeDtypeStruct((HPD, 2, chunk, HD), jnp.bfloat16),
        ],
        in_specs=[pl.BlockSpec(memory_space=pltpu.SMEM)] + [anywhere] * (count + 1),
        out_specs=[anywhere] * 2,
        scratch_shapes=[
            pltpu.VMEM((chunk, depth), jnp.bfloat16),
            pltpu.VMEM((HPD // BATCH, depth, BATCH * 3 * HD), jnp.bfloat16),
            pltpu.VMEM((HPD, 3, chunk, HD), jnp.bfloat16),
            pltpu.SemaphoreType.DMA((count,)),
            pltpu.SemaphoreType.DMA((HPD // BATCH,)),
            pltpu.SemaphoreType.DMA((2 * HPD,)),
        ],
        compiler_params=pltpu.CompilerParams(vmem_limit_bytes=24 * MIB),
        cost_estimate=pl.CostEstimate(flops=1, bytes_accessed=1, transcendentals=0),
    )(place, *pieces, weight)


def attention_body(batch, rounds, layers, slots, counts, strips, *refs):
    queries_in = refs[:rounds]
    sources = refs[rounds : 4 * rounds]
    out, query, keyvals, keys, values, query_sems, key_sems = refs[4 * rounds :]
    chunk = query.shape[1] // rounds
    copies = [[] for _ in range(BATCH)]
    for spot in range(BATCH):
        head = batch * BATCH + spot
        for i in range(rounds):
            for column in range(3):
                at = pl.ds(pl.multiple_of(strips[column * rounds + i] * chunk, chunk), chunk)
                copies[spot].append(
                    pltpu.make_async_copy(
                        sources[3 * i + column].at[head],
                        keyvals.at[spot, column, :, at],
                        key_sems.at[spot, 3 * i + column],
                    )
                )
            at = pl.ds(pl.multiple_of(strips[i] * chunk, chunk), chunk)
            copies[spot].append(
                pltpu.make_async_copy(
                    queries_in[i].at[head], query.at[spot, at], query_sems.at[spot, i]
                )
            )
    for some in copies:
        for copy in some:
            copy.start()

    def cells(layer, half):
        return [
            pl.ds(pl.multiple_of(((layer * TF + frame) * GH + half) * TH * TW, TH * TW), TH * TW)
            for frame in range(TF)
        ]

    def one_tile(spot, tile, carry):
        layer = tile // GH
        half = tile % GH

        def with_slots(count):
            for slot in range(count):
                found = slots[tile * NB + slot]
                column = found // (layers * GH)
                place = cells(found // GH % layers, found % GH)
                for kind, store in ((0, keys), (1, values)):
                    for frame, rows in enumerate(place):
                        start = slot * CELLS + frame * TH * TW
                        store[start : start + TH * TW] = keyvals[spot, column, kind, rows]
            queries = jnp.concatenate([query[spot, rows] for rows in cells(layer, half)], axis=0)
            results = []
            starts = list(range(0, CELLS, ROW_BLOCK))

            def scores_of(row):
                return lax.dot_general(
                    queries[row : row + ROW_BLOCK],
                    keys[: count * CELLS],
                    (((1,), (1,)), ((), ())),
                    preferred_element_type=jnp.float32,
                )

            ready = [scores_of(row) for row in starts[:AHEAD]]
            for i in range(len(starts)):
                if i + AHEAD < len(starts):
                    ready.append(scores_of(starts[i + AHEAD]))
                scores = ready[i]
                peak = jnp.max(scores, axis=1, keepdims=True)
                weights = jnp.exp2(scores * EXP2_SCALE - peak * EXP2_SCALE)
                denom = jnp.sum(weights, axis=1, keepdims=True)
                mixed = jnp.dot(
                    weights.astype(jnp.bfloat16),
                    values[: count * CELLS],
                    preferred_element_type=jnp.float32,
                )
                results.append(mixed / denom)
            result = jnp.concatenate(results, axis=0).astype(jnp.bfloat16)
            for frame, rows in enumerate(cells(layer, half)):
                out[spot, rows] = result[frame * TH * TW : (frame + 1) * TH * TW]

        for count in range(1, NB + 1):
            pl.when(counts[tile] == count)(functools.partial(with_slots, count))
        return carry

    for spot in range(BATCH):
        for copy in copies[spot]:
            copy.wait()
        lax.fori_loop(0, layers * GH, functools.partial(one_tile, spot), 0)


def attend(batch, slots, counts, strips, queries_in, sources):
    rounds = len(queries_in)
    chunk = queries_in[0].shape[1]
    tokens = rounds * chunk
    layers = tokens // (TF * GH * TH * TW)
    smem = pl.BlockSpec(memory_space=pltpu.SMEM)
    anywhere = pl.BlockSpec(memory_space=pl.ANY)
    return pl.pallas_call(
        functools.partial(attention_body, batch, rounds, layers),
        out_shape=jax.ShapeDtypeStruct((BATCH, tokens, HD), jnp.bfloat16),
        in_specs=[smem, smem, smem] + [anywhere] * (4 * rounds),
        out_specs=pl.BlockSpec(memory_space=pltpu.VMEM),
        scratch_shapes=[
            pltpu.VMEM((BATCH, tokens, HD), jnp.bfloat16),
            pltpu.VMEM((BATCH, 3, 2, tokens, HD), jnp.bfloat16),
            pltpu.VMEM((NB * CELLS, HD), jnp.bfloat16),
            pltpu.VMEM((NB * CELLS, HD), jnp.bfloat16),
            pltpu.SemaphoreType.DMA((BATCH, rounds)),
            pltpu.SemaphoreType.DMA((BATCH, 3 * rounds)),
        ],
        compiler_params=pltpu.CompilerParams(vmem_limit_bytes=24 * MIB),
        cost_estimate=pl.CostEstimate(flops=1, bytes_accessed=1, transcendentals=0),
    )(slots, counts, strips, *queries_in, *sources)


def output_body(rounds, rows, strips, *refs):
    batches = HPD // BATCH
    pieces = refs[: rounds * batches]
    w_own, w_got, w_also, gate, out, mixed, weight, sems, weight_sems = refs[rounds * batches :]
    part = rows * TW
    steps, _, step = weight.shape
    block = BATCH * HD
    own_half, own_clip = strips[rounds + 1], strips[rounds + 2]
    n = pl.program_id(0)

    @pl.when(n == 0)
    def _():
        copies = []
        for i in range(rounds):
            for spot in range(2 * HPD):
                batch, inner = spot // (2 * BATCH), spot % (2 * BATCH)
                copy = pltpu.make_async_copy(
                    pieces[i * batches + batch].at[inner],
                    mixed.at[pl.ds(i * 2 * part, 2 * part), pl.ds(spot * HD, HD)],
                    sems.at[i, spot],
                )
                copy.start()
                copies.append(copy)
        for k in range(steps):
            in_own = (k // (steps // 2)) == own_half
            columns = pl.ds(k % (steps // 2) * step, step)
            for batch in range(batches):
                for over_blk in range(2):
                    half = own_half ^ over_blk
                    group = batch * 2 + over_blk
                    target = weight.at[k, pl.ds(group * block, block)]
                    sem = weight_sems.at[k, group]
                    own_row = pl.multiple_of((half * batches + batch) * block, block)
                    far_row = batch * block

                    @pl.when(in_own)
                    def _():
                        pltpu.make_async_copy(
                            w_own.at[pl.ds(own_row, block), columns], target, sem
                        ).start()

                    @pl.when(jnp.logical_and(jnp.logical_not(in_own), half == own_clip))
                    def _():
                        pltpu.make_async_copy(
                            w_got.at[pl.ds(far_row, block), columns], target, sem
                        ).start()

                    @pl.when(jnp.logical_and(jnp.logical_not(in_own), half != own_clip))
                    def _():
                        pltpu.make_async_copy(
                            w_also.at[pl.ds(far_row, block), columns], target, sem
                        ).start()

        for copy in copies:
            copy.wait()

    for group in range(2 * batches):
        pltpu.make_async_copy(
            w_own.at[pl.ds(0, block), pl.ds(0, step)],
            weight.at[n, pl.ds(group * block, block)],
            weight_sems.at[n, group],
        ).wait()
    product = jnp.dot(mixed[...], weight[n], preferred_element_type=jnp.float32) * gate[...]
    ordered = strips[rounds] == 0
    for i in range(rounds):
        strip = strips[i]
        for row in range(rows):
            base = i * 2 * part + row * TW
            near, far = product[base : base + TW], product[base + part : base + part + TW]
            both = jnp.concatenate(
                [jnp.where(ordered, near, far), jnp.where(ordered, far, near)], axis=0
            )
            out[row, strip] = both.astype(jnp.bfloat16)


def project_out(strips, pieces, weights, gate, rows):
    rounds = len(pieces) // (HPD // BATCH)
    depth, width = weights[0].shape[0], gate.shape[1]
    step = 512
    steps = width // step
    anywhere = pl.BlockSpec(memory_space=pl.ANY)
    return pl.pallas_call(
        lambda strips_ref, *refs: output_body(rounds, rows, strips_ref, *refs),
        out_shape=jax.ShapeDtypeStruct((rows, rounds, 2 * TW, width), jnp.bfloat16),
        grid=(steps,),
        in_specs=[pl.BlockSpec(memory_space=pltpu.SMEM)]
        + [anywhere] * (len(pieces) + 3)
        + [pl.BlockSpec((1, step), lambda n: (0, n))],
        out_specs=pl.BlockSpec((rows, rounds, 2 * TW, step), lambda n: (0, 0, 0, n)),
        scratch_shapes=[
            pltpu.VMEM((rounds * rows * 2 * TW, depth), jnp.bfloat16),
            pltpu.VMEM((steps, depth, step), jnp.bfloat16),
            pltpu.SemaphoreType.DMA((rounds, 2 * HPD)),
            pltpu.SemaphoreType.DMA((steps, 2 * (HPD // BATCH))),
        ],
        compiler_params=pltpu.CompilerParams(vmem_limit_bytes=28 * MIB),
    )(strips, *pieces, *weights, gate)


def local(modulated, mod_gate, w_qkv, w_out, kv_tiles, kv_count):
    tok_rows, depth = modulated.shape
    seq_count = lax.axis_size("seq")
    rounds = seq_count // 2
    rows = tok_rows // (seq_count * TW)
    part = rows * TW
    strip_tokens = rounds * 4 * part
    layers = strip_tokens // (TF * GH * TH * TW)
    seq_index = lax.axis_index("seq")
    strip, half = seq_index // 2, seq_index % 2
    blk, clip = lax.axis_index("blk"), lax.axis_index("clip")

    def swap(array, over_blk, over_clip):
        return permuted(
            array, seq_count, lambda s, h, b, c: (s, h, b ^ over_blk, c ^ over_clip)
        )

    def regroup(array, distance, flip=0):
        return permuted(array, seq_count, lambda s, h, b, c: (s ^ distance, c, b, h ^ flip))

    by_strip = modulated.reshape(rows, rounds, 2, TW, depth)
    order = jnp.stack(
        [
            (clip ^ flip) * 2 + (blk ^ over_blk)
            for flip in range(2)
            for over_blk in range(2)
        ]
    ).astype(jnp.int32)
    units = [(i, flip) for i in range(rounds) for flip in range(2)]
    near = len(units) // 2
    pieces, mirrors = {}, {}

    def fetch(n, *others):
        i, flip = units[n]
        sent = lax.dynamic_index_in_dim(by_strip, strip ^ i, 1, keepdims=False)
        sent = lax.dynamic_index_in_dim(sent, half ^ flip, 1, keepdims=False)
        sent = sent.reshape(part, depth)
        pieces[n] = regroup(after(sent, *others) if others else sent, i, flip)

    queries_in, own = [None] * rounds, [None] * rounds
    outers, inners = [None] * rounds, [None] * rounds
    for step in range(len(units)):
        n = step // 2 + near * (step % 2)
        fetch(n, *([pieces[n - 1]] if n % near else []))
    last_piece = pieces[len(units) - 1]

    def outward(s, h, b, c):
        goal = s + (1 if c else -1)
        return (goal, h, b, 1 - c) if 0 <= goal < rounds else None

    ready, ready_at, previous = [], [], None
    for step in range(len(units)):
        n = step // 2 + near * (step % 2)
        held = [previous] if step else []
        if step >= 4:
            held.append(ready[(step - 4) // 4 * 2 + min(step % 4, 1)])
        mirrors[n] = swap(after(pieces[n], *held) if held else pieces[n], 1, 0)
        previous = mirrors[n]
        if n % 2:
            i = n // 2
            mirror = mirrors[n]
            if step >= len(units) - 2:
                mirror = after(mirror, outers[ready_at[-2]])
            if step == len(units) - 1:
                mirror = after(mirror, ready[-1])
                last = mirror
            quad = [pieces[n - 1], mirrors[n - 1], pieces[n], mirror]
            if part % 16:
                quad = [
                    jnp.take(jnp.stack(quad), jnp.argsort(order), axis=0).reshape(4 * part, depth)
                ]
            queries_in[i], own[i] = project(
                order * 0 if part % 16 else order, quad, w_qkv
            )
            ready.append(queries_in[i])
            ready_at.append(i)
            keyval = own[i]
            if step < len(units) - 2:
                keyval = after(keyval, last_piece)
            outers[i], inners[i] = permuted(keyval, seq_count, outward), swap(keyval, 0, 1)

    lists = jnp.concatenate([kv_tiles, kv_count[:, None]], axis=1)
    lists = regroup(lists, 0).reshape(layers * GH, seq_count, NB + 1)
    column = strip * 2 + clip
    lists = lax.dynamic_index_in_dim(lists, column, 1, keepdims=False)
    counts = lists[:, NB]
    tiles = lists[:, :NB]
    side = tiles % seq_count - column
    from_outer = (side == 1) == (clip == 1)
    source = jnp.where(side == 0, 0, jnp.where(from_outer, 1, 2))
    slots = (source * (layers * GH) + tiles // seq_count).reshape(-1)

    sources = [some[i] for i in range(rounds) for some in (own, outers, inners)]
    outer_strip = strip + 2 * clip - 1
    spots = jnp.stack(
        [strip ^ i for i in range(rounds)]
        + [(outer_strip ^ i) & (rounds - 1) for i in range(rounds)]
        + [strip ^ i for i in range(rounds)]
    ).astype(jnp.int32)

    w_half = w_out.shape[0] // 2
    w_sent = lax.dynamic_slice_in_dim(w_out, clip * w_half, w_half, axis=0)
    w_sent = after(w_sent, last)
    w_got = swap(w_sent, 1, 0)
    w_also = swap(w_got, 0, 1)

    returned = [[None] * (HPD // BATCH) for _ in range(rounds)]
    cores, crosses = [], []
    for batch in range(HPD // BATCH):
        queries = list(queries_in)
        if batch:
            queries[0] = after(queries[0], crosses[0] if batch > 1 else cores[0])
        result = attend(batch, slots, counts, spots, queries, sources)
        result = result.reshape(BATCH, rounds, 2, 2, part, HD)
        kept = lax.dynamic_index_in_dim(result, clip, 2, keepdims=False)
        given = lax.dynamic_index_in_dim(result, 1 - clip, 2, keepdims=False)
        cores.append(swap(given, 0, 1))
        both = jnp.stack([kept, cores[-1]], axis=3)
        kept = lax.dynamic_index_in_dim(both, blk, 2, keepdims=False)
        given = lax.dynamic_index_in_dim(both, 1 - blk, 2, keepdims=False)
        crosses.append(swap(given, 1, 0))
        group = jnp.concatenate([kept, crosses[-1]], axis=0)
        for i in range(rounds):
            sent = lax.dynamic_index_in_dim(group, strip ^ i, 1, keepdims=False)
            returned[i][batch] = regroup(sent.reshape(2 * BATCH, 2 * part, HD), i)

    strips = jnp.stack([strip ^ i for i in range(rounds)] + [half, blk, clip]).astype(jnp.int32)
    flat = [piece for some in returned for piece in some]
    out = project_out(strips, flat, (w_out, w_got, w_also), mod_gate.reshape(1, -1), rows)
    return out.reshape(tok_rows, -1)


def solution(mesh):
    return jax.shard_map(
        local,
        mesh=mesh,
        in_specs=(
            P(("clip", "seq", "blk"), None),
            P("clip"),
            P(None, "blk"),
            P(None, "blk"),
            P("clip", None),
            P("clip"),
        ),
        out_specs=P(("clip", "seq", "blk"), None),
        check_vma=False,
    )
```

```python
import functools
import math

import jax
import jax.numpy as jnp
from jax import lax
from jax.experimental import pallas as pl
from jax.experimental.pallas import tpu as pltpu
from jax.sharding import PartitionSpec as P

HD = 128
NH = 12
TF = 6
TH = 8
TW = 8
NB = 6
GH = 2
CELLS = TF * TH * TW
AXES = ("seq", "blk", "clip")
HPD = NH // 2
PAIR = 2
BATCHES = ((0, 4), (4, 2))
EXP2_SCALE = math.log2(math.e) / math.sqrt(HD)
MIB = 1 << 20
ROW_BLOCK = 192
AHEAD = 1


def permuted(array, seq_count, target):
    pairs = []
    for seq in range(seq_count):
        for blk in range(2):
            for clip in range(2):
                goal = target(seq // 2, seq % 2, blk, clip)
                if goal is not None:
                    strip, half, blk_to, clip_to = goal
                    pairs.append(
                        ((seq * 2 + blk) * 2 + clip, ((strip * 2 + half) * 2 + blk_to) * 2 + clip_to)
                    )
    return lax.ppermute(array, AXES, pairs)


def after(array, *others):
    return lax.optimization_barrier((array,) + others)[0]


def projection_body(count, spot_out, shared, place, *refs):
    pieces, weight = refs[:count], refs[count]
    query, keyval = refs[count + 1 + shared : count + 3 + shared]
    tokens, columns, blocks, token_sem, weight_sem, out_sem = refs[count + 3 + shared :]
    piece_rows = pieces[0].shape[0]
    loads = []
    for i in range(count):
        start = pl.multiple_of(place[i] * piece_rows, piece_rows)
        loads.append(
            pltpu.make_async_copy(
                pieces[i], tokens.at[pl.ds(start, piece_rows)], token_sem.at[i]
            )
        )
    width = PAIR * 3 * HD
    streams = []
    for batch in range(HPD // PAIR):
        streams.append(
            pltpu.make_async_copy(
                weight.at[:, pl.ds(batch * width, width)], columns.at[batch], weight_sem.at[batch]
            )
        )
    for copy in loads:
        copy.start()
    for copy in streams:
        copy.start()
    for copy in loads:
        copy.wait()
    stores = []
    for batch in range(HPD // PAIR):
        streams[batch].wait()
        total = jnp.dot(tokens[...], columns[batch], preferred_element_type=jnp.float32)
        for spot in range(PAIR):
            head = batch * PAIR + spot
            for kind in range(3):
                start = (spot * 3 + kind) * HD
                blocks[head, kind] = total[:, start : start + HD].astype(jnp.bfloat16)
            for target, some in (
                (query.at[spot_out[0], head], blocks.at[head, 0]),
                (keyval.at[spot_out[1], head], blocks.at[head, pl.ds(1, 2)]),
            ):
                copy = pltpu.make_async_copy(some, target, out_sem.at[len(stores)])
                copy.start()
                stores.append(copy)
    for copy in stores:
        copy.wait()


def project(place, pieces, weight, spot_out, sizes, query, keyval):
    count = len(pieces)
    given = [array for array in (query, keyval) if array is not None]
    aliases = {}
    for array, out in ((query, 0), (keyval, 1)):
        if array is not None:
            aliases[count + 2 + len(aliases)] = out
    piece_rows, depth = pieces[0].shape
    chunk = count * piece_rows
    hbm = pl.BlockSpec(memory_space=pltpu.HBM)
    return pl.pallas_call(
        functools.partial(projection_body, count, spot_out, len(given)),
        out_shape=[
            jax.ShapeDtypeStruct((sizes[0], HPD, chunk, HD), jnp.bfloat16),
            jax.ShapeDtypeStruct((sizes[1], HPD, 2, chunk, HD), jnp.bfloat16),
        ],
        in_specs=[pl.BlockSpec(memory_space=pltpu.SMEM)] + [hbm] * (count + 1 + len(given)),
        out_specs=[hbm] * 2,
        input_output_aliases=aliases,
        scratch_shapes=[
            pltpu.VMEM((chunk, depth), jnp.bfloat16),
            pltpu.VMEM((HPD // PAIR, depth, PAIR * 3 * HD), jnp.bfloat16),
            pltpu.VMEM((HPD, 3, chunk, HD), jnp.bfloat16),
            pltpu.SemaphoreType.DMA((count,)),
            pltpu.SemaphoreType.DMA((HPD // PAIR,)),
            pltpu.SemaphoreType.DMA((2 * HPD,)),
        ],
        compiler_params=pltpu.CompilerParams(vmem_limit_bytes=40 * MIB),
        cost_estimate=pl.CostEstimate(flops=1, bytes_accessed=1, transcendentals=0),
    )(place, *pieces, weight, *given)


def attention_body(first, span, homes, rounds, layers, slots, counts, strips, *refs):
    count = 1 + 3 * (1 + max(group for group, _ in homes))
    queries_in, sources = refs[0], refs[1:count]
    out, query, keyvals, keys, values, query_sems, key_sems = refs[count:]
    chunk = query.shape[1] // rounds
    copies = [[] for _ in range(span)]
    for spot in range(span):
        head = first + spot
        for i in range(rounds):
            for column in range(3):
                at = pl.ds(pl.multiple_of(strips[column * rounds + i] * chunk, chunk), chunk)
                copies[spot].append(
                    pltpu.make_async_copy(
                        sources[3 * homes[i][0] + column].at[homes[i][1], head],
                        keyvals.at[spot, column, :, at],
                        key_sems.at[spot, 3 * i + column],
                    )
                )
            at = pl.ds(pl.multiple_of(strips[i] * chunk, chunk), chunk)
            copies[spot].append(
                pltpu.make_async_copy(
                    queries_in.at[i, head], query.at[spot, at], query_sems.at[spot, i]
                )
            )
    for some in copies:
        for copy in some:
            copy.start()

    def cells(layer, half):
        return [
            pl.ds(pl.multiple_of(((layer * TF + frame) * GH + half) * TH * TW, TH * TW), TH * TW)
            for frame in range(TF)
        ]

    def one_tile(spot, tile, carry):
        layer = tile // GH
        half = tile % GH

        def with_slots(count):
            for slot in range(count):
                found = slots[tile * NB + slot]
                column = found // (layers * GH)
                place = cells(found // GH % layers, found % GH)
                for kind, store in ((0, keys), (1, values)):
                    for frame, rows in enumerate(place):
                        start = slot * CELLS + frame * TH * TW
                        store[start : start + TH * TW] = keyvals[spot, column, kind, rows]
            queries = jnp.concatenate([query[spot, rows] for rows in cells(layer, half)], axis=0)
            results = []
            starts = list(range(0, CELLS, ROW_BLOCK))

            def scores_of(row):
                return lax.dot_general(
                    queries[row : row + ROW_BLOCK],
                    keys[: count * CELLS],
                    (((1,), (1,)), ((), ())),
                    preferred_element_type=jnp.float32,
                )

            ready = [scores_of(row) for row in starts[:AHEAD]]
            for i in range(len(starts)):
                if i + AHEAD < len(starts):
                    ready.append(scores_of(starts[i + AHEAD]))
                scores = ready[i]
                peak = jnp.max(scores, axis=1, keepdims=True)
                weights = jnp.exp2(scores * EXP2_SCALE - peak * EXP2_SCALE)
                denom = jnp.sum(weights, axis=1, keepdims=True)
                mixed = jnp.dot(
                    weights.astype(jnp.bfloat16),
                    values[: count * CELLS],
                    preferred_element_type=jnp.float32,
                )
                results.append(mixed / denom)
            result = jnp.concatenate(results, axis=0).astype(jnp.bfloat16)
            for frame, rows in enumerate(cells(layer, half)):
                out[spot, rows] = result[frame * TH * TW : (frame + 1) * TH * TW]

        for count in range(1, NB + 1):
            pl.when(counts[tile] == count)(functools.partial(with_slots, count))
        return carry

    for spot in range(span):
        for copy in copies[spot]:
            copy.wait()
        lax.fori_loop(0, layers * GH, functools.partial(one_tile, spot), 0)


def attend(first, span, homes, slots, counts, strips, queries_in, sources):
    rounds, _, chunk, _ = queries_in.shape
    tokens = rounds * chunk
    layers = tokens // (TF * GH * TH * TW)
    smem = pl.BlockSpec(memory_space=pltpu.SMEM)
    anywhere = pl.BlockSpec(memory_space=pl.ANY)
    hbm = pl.BlockSpec(memory_space=pltpu.HBM)
    return pl.pallas_call(
        functools.partial(attention_body, first, span, homes, rounds, layers),
        out_shape=jax.ShapeDtypeStruct((span, tokens, HD), jnp.bfloat16),
        in_specs=[smem, smem, smem] + [hbm] + [anywhere] * len(sources),
        out_specs=pl.BlockSpec(memory_space=pltpu.VMEM),
        scratch_shapes=[
            pltpu.VMEM((span, tokens, HD), jnp.bfloat16),
            pltpu.VMEM((span, 3, 2, tokens, HD), jnp.bfloat16),
            pltpu.VMEM((NB * CELLS, HD), jnp.bfloat16),
            pltpu.VMEM((NB * CELLS, HD), jnp.bfloat16),
            pltpu.SemaphoreType.DMA((span, rounds)),
            pltpu.SemaphoreType.DMA((span, 3 * rounds)),
        ],
        compiler_params=pltpu.CompilerParams(vmem_limit_bytes=60 * MIB),
        cost_estimate=pl.CostEstimate(flops=1, bytes_accessed=1, transcendentals=0),
    )(slots, counts, strips, queries_in, *sources)


def output_body(rounds, rows, strips, *refs):
    count = rounds * len(BATCHES) * 2
    pieces = refs[:count]
    w_own, w_got, w_also, gate, out, mixed, weight, sems, weight_sems = refs[count:]
    part = rows * TW
    steps, _, step = weight.shape
    own_half, own_clip = strips[rounds + 1], strips[rounds + 2]
    n = pl.program_id(0)

    @pl.when(n == 0)
    def _():
        copies = []
        for i in range(rounds):
            for batch, (first, span) in enumerate(BATCHES):
                for spot in range(2 * span):
                    column = 2 * first + spot
                    copy = pltpu.make_async_copy(
                        pieces[(i * len(BATCHES) + batch) * 2 + spot // span].at[spot % span],
                        mixed.at[pl.ds(i * 2 * part, 2 * part), pl.ds(column * HD, HD)],
                        sems.at[i, column],
                    )
                    copy.start()
                    copies.append(copy)
        for k in range(steps):
            in_own = (k // (steps // 2)) == own_half
            columns = pl.ds(k % (steps // 2) * step, step)
            for batch, (first, span) in enumerate(BATCHES):
                block = span * HD
                for over_blk in range(2):
                    half = own_half ^ over_blk
                    target = weight.at[k, pl.ds((2 * first + over_blk * span) * HD, block)]
                    sem = weight_sems.at[k, batch * 2 + over_blk]
                    own_row = pl.multiple_of((half * HPD + first) * HD, HD)
                    far_row = first * HD

                    @pl.when(in_own)
                    def _():
                        pltpu.make_async_copy(
                            w_own.at[pl.ds(own_row, block), columns], target, sem
                        ).start()

                    @pl.when(jnp.logical_and(jnp.logical_not(in_own), half == own_clip))
                    def _():
                        pltpu.make_async_copy(
                            w_got.at[pl.ds(far_row, block), columns], target, sem
                        ).start()

                    @pl.when(jnp.logical_and(jnp.logical_not(in_own), half != own_clip))
                    def _():
                        pltpu.make_async_copy(
                            w_also.at[pl.ds(far_row, block), columns], target, sem
                        ).start()

        for copy in copies:
            copy.wait()

    for batch, (first, span) in enumerate(BATCHES):
        for over_blk in range(2):
            pltpu.make_async_copy(
                w_own.at[pl.ds(0, span * HD), pl.ds(0, step)],
                weight.at[n, pl.ds((2 * first + over_blk * span) * HD, span * HD)],
                weight_sems.at[n, batch * 2 + over_blk],
            ).wait()
    product = jnp.dot(mixed[...], weight[n], preferred_element_type=jnp.float32) * gate[...]
    ordered = strips[rounds] == 0
    for i in range(rounds):
        strip = strips[i]
        for row in range(rows):
            base = i * 2 * part + row * TW
            near, far = product[base : base + TW], product[base + part : base + part + TW]
            both = jnp.concatenate(
                [jnp.where(ordered, near, far), jnp.where(ordered, far, near)], axis=0
            )
            out[row, strip] = both.astype(jnp.bfloat16)


def project_out(strips, pieces, weights, gate, rows):
    rounds = len(pieces) // (2 * len(BATCHES))
    depth, width = weights[0].shape[0], gate.shape[1]
    step = 512
    steps = width // step
    anywhere = pl.BlockSpec(memory_space=pl.ANY)
    return pl.pallas_call(
        lambda strips_ref, *refs: output_body(rounds, rows, strips_ref, *refs),
        out_shape=jax.ShapeDtypeStruct((rows, rounds, 2 * TW, width), jnp.bfloat16),
        grid=(steps,),
        in_specs=[pl.BlockSpec(memory_space=pltpu.SMEM)]
        + [anywhere] * (len(pieces) + 3)
        + [pl.BlockSpec((1, step), lambda n: (0, n))],
        out_specs=pl.BlockSpec((rows, rounds, 2 * TW, step), lambda n: (0, 0, 0, n)),
        scratch_shapes=[
            pltpu.VMEM((rounds * rows * 2 * TW, depth), jnp.bfloat16),
            pltpu.VMEM((steps, depth, step), jnp.bfloat16),
            pltpu.SemaphoreType.DMA((rounds, 2 * HPD)),
            pltpu.SemaphoreType.DMA((steps, 2 * len(BATCHES))),
        ],
        compiler_params=pltpu.CompilerParams(vmem_limit_bytes=28 * MIB),
    )(strips, *pieces, *weights, gate)


def local(modulated, mod_gate, w_qkv, w_out, kv_tiles, kv_count):
    tok_rows, depth = modulated.shape
    seq_count = lax.axis_size("seq")
    rounds = seq_count // 2
    rows = tok_rows // (seq_count * TW)
    part = rows * TW
    strip_tokens = rounds * 4 * part
    layers = strip_tokens // (TF * GH * TH * TW)
    seq_index = lax.axis_index("seq")
    strip, half = seq_index // 2, seq_index % 2
    blk, clip = lax.axis_index("blk"), lax.axis_index("clip")

    def swap(array, over_blk, over_clip):
        return permuted(
            array, seq_count, lambda s, h, b, c: (s, h, b ^ over_blk, c ^ over_clip)
        )

    def regroup(array, distance, flip=0):
        return permuted(array, seq_count, lambda s, h, b, c: (s ^ distance, c, b, h ^ flip))

    by_strip = modulated.reshape(rows, rounds, 2, TW, depth)
    order = jnp.stack(
        [
            (clip ^ flip) * 2 + (blk ^ over_blk)
            for flip in range(2)
            for over_blk in range(2)
        ]
    ).astype(jnp.int32)
    units = [(i, flip) for i in range(rounds) for flip in range(2)]
    near = len(units) // 2
    w_half = w_out.shape[0] // 2
    live = {"w": lax.dynamic_slice_in_dim(w_out, clip * w_half, w_half, axis=0)}
    for n, (i, flip) in enumerate(units):
        sent = lax.dynamic_index_in_dim(by_strip, strip ^ i, 1, keepdims=False)
        sent = lax.dynamic_index_in_dim(sent, half ^ flip, 1, keepdims=False)
        live["send", n] = sent.reshape(part, depth)

    def outward(s, h, b, c):
        goal = s + (1 if c else -1)
        return (goal, h, b, 1 - c) if 0 <= goal < rounds else None

    def halo(group):
        live["outer", group] = permuted(live["own", group], seq_count, outward)
        live["inner", group] = swap(live["own", group], 0, 1)

    last_step = near + 1
    when = {}
    for i in range(rounds):
        when[i] = min(2 * i + 2 if i < rounds // 2 else 2 * i - near + 4, last_step)
    members = [
        [i for i in range(rounds) if when[i] < near],
        [i for i in range(rounds) if when[i] == near],
        [i for i in range(rounds) if when[i] == last_step],
    ]
    homes = tuple(
        next((g, some.index(i)) for g, some in enumerate(members) if i in some)
        for i in range(rounds)
    )
    for step in range(last_step + 1):
        before = dict(live)
        fetched = [near + step] if step < near else []
        fetched += [0, 1] if step == 0 else [step + 1] if step + 1 < near else []
        if step == 1:
            mirrored = [0, 1]
        elif 2 <= step < near:
            mirrored = [near + step - 2, step]
        else:
            mirrored = [2 * near - 2, 2 * near - 1] if step == near else []
        for n in fetched:
            live["piece", n] = regroup(live.pop(("send", n)), *units[n])
        for n in mirrored:
            live["mirror", n] = swap(before["piece", n], 1, 0)
        if step == near:
            halo(0)
        if step == last_step:
            halo(1)
            w_got = swap(live.pop("w"), 1, 0)
        for i in range(rounds):
            if when[i] != step:
                continue
            quad = [live.pop((kind, 2 * i + f)) for f in range(2) for kind in ("piece", "mirror")]
            if part % 16:
                quad = [
                    jnp.take(jnp.stack(quad), jnp.argsort(order), axis=0).reshape(4 * part, depth)
                ]
            group, spot = homes[i]
            live["query"], live["own", group] = project(
                order * 0 if part % 16 else order,
                quad,
                w_qkv,
                (i, spot),
                (rounds, len(members[group])),
                live.get("query"),
                live.get(("own", group)),
            )
        if step < last_step:
            names = list(live)
            live = dict(zip(names, lax.optimization_barrier([live[name] for name in names])))
    halo(2)
    query = live["query"]
    sources = [live[kind, group] for group in range(3) for kind in ("own", "outer", "inner")]

    lists = jnp.concatenate([kv_tiles, kv_count[:, None]], axis=1)
    lists = regroup(lists, 0).reshape(layers * GH, seq_count, NB + 1)
    column = strip * 2 + clip
    lists = lax.dynamic_index_in_dim(lists, column, 1, keepdims=False)
    counts = lists[:, NB]
    tiles = lists[:, :NB]
    side = tiles % seq_count - column
    from_outer = (side == 1) == (clip == 1)
    source = jnp.where(side == 0, 0, jnp.where(from_outer, 1, 2))
    slots = (source * (layers * GH) + tiles // seq_count).reshape(-1)

    outer_strip = strip + 2 * clip - 1
    spots = jnp.stack(
        [strip ^ i for i in range(rounds)]
        + [(outer_strip ^ i) & (rounds - 1) for i in range(rounds)]
        + [strip ^ i for i in range(rounds)]
    ).astype(jnp.int32)


    returned, core = {}, None
    for batch, (first, span) in enumerate(BATCHES):
        asked = after(query, core) if batch else query
        result = attend(first, span, homes, slots, counts, spots, asked, sources)
        result = result.reshape(span, rounds, 2, 2, part, HD)
        kept = lax.dynamic_index_in_dim(result, clip, 2, keepdims=False)
        given = lax.dynamic_index_in_dim(result, 1 - clip, 2, keepdims=False)
        core = swap(given, 0, 1)
        if not batch:
            w_also = swap(after(w_got, core), 0, 1)
        both = jnp.stack([kept, core], axis=3)
        for i in range(rounds):
            for over in range(2):
                sent = lax.dynamic_index_in_dim(both, blk ^ over, 2, keepdims=False)
                sent = lax.dynamic_index_in_dim(sent, strip ^ i, 1, keepdims=False)
                returned[batch, i, over] = permuted(
                    sent.reshape(span, 2 * part, HD),
                    seq_count,
                    lambda s, h, b, c: (s ^ i, c, b ^ over, h),
                )

    strips = jnp.stack([strip ^ i for i in range(rounds)] + [half, blk, clip]).astype(jnp.int32)
    flat = [
        returned[batch, i, over]
        for i in range(rounds)
        for batch in range(len(BATCHES))
        for over in range(2)
    ]
    out = project_out(strips, flat, (w_out, w_got, w_also), mod_gate.reshape(1, -1), rows)
    return out.reshape(tok_rows, -1)


def solution(mesh):
    return jax.shard_map(
        local,
        mesh=mesh,
        in_specs=(
            P(("clip", "seq", "blk"), None),
            P("clip"),
            P(None, "blk"),
            P(None, "blk"),
            P("clip", None),
            P("clip"),
        ),
        out_specs=P(("clip", "seq", "blk"), None),
        check_vma=False,
    )
```

```python
import functools
import math

import jax
import jax.numpy as jnp
from jax import lax
from jax.experimental import pallas as pl
from jax.experimental.pallas import tpu as pltpu
from jax.sharding import PartitionSpec as P

HD = 128
NH = 12
TF = 6
TH = 8
TW = 8
NB = 6
GH = 2
CELLS = TF * TH * TW
AXES = ("seq", "blk", "clip")
HPD = NH // 2
PAIR = 2
BATCHES = ((0, 3), (3, 3))
EXP2_SCALE = math.log2(math.e) / math.sqrt(HD)
MIB = 1 << 20
ROW_BLOCK = 192
AHEAD = 1


def permuted(array, seq_count, target):
    pairs = []
    for seq in range(seq_count):
        for blk in range(2):
            for clip in range(2):
                goal = target(seq // 2, seq % 2, blk, clip)
                if goal is not None:
                    strip, half, blk_to, clip_to = goal
                    pairs.append(
                        ((seq * 2 + blk) * 2 + clip, ((strip * 2 + half) * 2 + blk_to) * 2 + clip_to)
                    )
    return lax.ppermute(array, AXES, pairs)


def after(array, *others):
    return lax.optimization_barrier((array,) + others)[0]


def projection_body(count, spot_out, shared, place, *refs):
    pieces, weight = refs[:count], refs[count]
    query, keyval = refs[count + 1 + shared : count + 3 + shared]
    tokens, columns, blocks, token_sem, weight_sem, out_sem = refs[count + 3 + shared :]
    piece_rows = pieces[0].shape[0]
    loads = []
    for i in range(count):
        start = pl.multiple_of(place[i] * piece_rows, piece_rows)
        loads.append(
            pltpu.make_async_copy(
                pieces[i], tokens.at[pl.ds(start, piece_rows)], token_sem.at[i]
            )
        )
    width = PAIR * 3 * HD
    streams = []
    for batch in range(HPD // PAIR):
        streams.append(
            pltpu.make_async_copy(
                weight.at[:, pl.ds(batch * width, width)], columns.at[batch], weight_sem.at[batch]
            )
        )
    for copy in loads:
        copy.start()
    for copy in streams:
        copy.start()
    for copy in loads:
        copy.wait()
    stores = []
    for batch in range(HPD // PAIR):
        streams[batch].wait()
        total = jnp.dot(tokens[...], columns[batch], preferred_element_type=jnp.float32)
        for spot in range(PAIR):
            head = batch * PAIR + spot
            for kind in range(3):
                start = (spot * 3 + kind) * HD
                blocks[head, kind] = total[:, start : start + HD].astype(jnp.bfloat16)
            for target, some in (
                (query.at[spot_out[0], head], blocks.at[head, 0]),
                (keyval.at[spot_out[1], head], blocks.at[head, pl.ds(1, 2)]),
            ):
                copy = pltpu.make_async_copy(some, target, out_sem.at[len(stores)])
                copy.start()
                stores.append(copy)
    for copy in stores:
        copy.wait()


def project(place, pieces, weight, spot_out, sizes, query, keyval):
    count = len(pieces)
    given = [array for array in (query, keyval) if array is not None]
    aliases = {}
    for array, out in ((query, 0), (keyval, 1)):
        if array is not None:
            aliases[count + 2 + len(aliases)] = out
    piece_rows, depth = pieces[0].shape
    chunk = count * piece_rows
    hbm = pl.BlockSpec(memory_space=pltpu.HBM)
    return pl.pallas_call(
        functools.partial(projection_body, count, spot_out, len(given)),
        out_shape=[
            jax.ShapeDtypeStruct((sizes[0], HPD, chunk, HD), jnp.bfloat16),
            jax.ShapeDtypeStruct((sizes[1], HPD, 2, chunk, HD), jnp.bfloat16),
        ],
        in_specs=[pl.BlockSpec(memory_space=pltpu.SMEM)] + [hbm] * (count + 1 + len(given)),
        out_specs=[hbm] * 2,
        input_output_aliases=aliases,
        scratch_shapes=[
            pltpu.VMEM((chunk, depth), jnp.bfloat16),
            pltpu.VMEM((HPD // PAIR, depth, PAIR * 3 * HD), jnp.bfloat16),
            pltpu.VMEM((HPD, 3, chunk, HD), jnp.bfloat16),
            pltpu.SemaphoreType.DMA((count,)),
            pltpu.SemaphoreType.DMA((HPD // PAIR,)),
            pltpu.SemaphoreType.DMA((2 * HPD,)),
        ],
        compiler_params=pltpu.CompilerParams(vmem_limit_bytes=60 * MIB),
        cost_estimate=pl.CostEstimate(flops=1, bytes_accessed=1, transcendentals=0),
    )(place, *pieces, weight, *given)


def attention_body(first, span, homes, rounds, layers, slots, counts, strips, *refs):
    count = 1 + 3 * (1 + max(group for group, _ in homes))
    queries_in, sources = refs[0], refs[1:count]
    out, query, keyvals, keys, values, query_sems, key_sems = refs[count:]
    chunk = query.shape[1] // rounds
    copies = [[] for _ in range(span)]
    for spot in range(span):
        head = first + spot
        for i in range(rounds):
            for column in range(3):
                at = pl.ds(pl.multiple_of(strips[column * rounds + i] * chunk, chunk), chunk)
                copies[spot].append(
                    pltpu.make_async_copy(
                        sources[3 * homes[i][0] + column].at[homes[i][1], head],
                        keyvals.at[spot, column, :, at],
                        key_sems.at[spot, 3 * i + column],
                    )
                )
            at = pl.ds(pl.multiple_of(strips[i] * chunk, chunk), chunk)
            copies[spot].append(
                pltpu.make_async_copy(
                    queries_in.at[i, head], query.at[spot, at], query_sems.at[spot, i]
                )
            )
    for some in copies:
        for copy in some:
            copy.start()

    def cells(layer, half):
        return [
            pl.ds(pl.multiple_of(((layer * TF + frame) * GH + half) * TH * TW, TH * TW), TH * TW)
            for frame in range(TF)
        ]

    def one_tile(spot, tile, carry):
        layer = tile // GH
        half = tile % GH

        def with_slots(count):
            for slot in range(count):
                found = slots[tile * NB + slot]
                column = found // (layers * GH)
                place = cells(found // GH % layers, found % GH)
                for kind, store in ((0, keys), (1, values)):
                    for frame, rows in enumerate(place):
                        start = slot * CELLS + frame * TH * TW
                        store[start : start + TH * TW] = keyvals[spot, column, kind, rows]
            queries = jnp.concatenate([query[spot, rows] for rows in cells(layer, half)], axis=0)
            results = []
            starts = list(range(0, CELLS, ROW_BLOCK))

            def scores_of(row):
                return lax.dot_general(
                    queries[row : row + ROW_BLOCK],
                    keys[: count * CELLS],
                    (((1,), (1,)), ((), ())),
                    preferred_element_type=jnp.float32,
                )

            ready = [scores_of(row) for row in starts[:AHEAD]]
            for i in range(len(starts)):
                if i + AHEAD < len(starts):
                    ready.append(scores_of(starts[i + AHEAD]))
                scores = ready[i]
                peak = jnp.max(scores, axis=1, keepdims=True)
                weights = jnp.exp2(scores * EXP2_SCALE - peak * EXP2_SCALE)
                denom = jnp.sum(weights, axis=1, keepdims=True)
                mixed = jnp.dot(
                    weights.astype(jnp.bfloat16),
                    values[: count * CELLS],
                    preferred_element_type=jnp.float32,
                )
                results.append(mixed / denom)
            result = jnp.concatenate(results, axis=0).astype(jnp.bfloat16)
            for frame, rows in enumerate(cells(layer, half)):
                out[spot, rows] = result[frame * TH * TW : (frame + 1) * TH * TW]

        for count in range(1, NB + 1):
            pl.when(counts[tile] == count)(functools.partial(with_slots, count))
        return carry

    for spot in range(span):
        for copy in copies[spot]:
            copy.wait()
        lax.fori_loop(0, layers * GH, functools.partial(one_tile, spot), 0)


def attend(first, span, homes, slots, counts, strips, queries_in, sources):
    rounds, _, chunk, _ = queries_in.shape
    tokens = rounds * chunk
    layers = tokens // (TF * GH * TH * TW)
    smem = pl.BlockSpec(memory_space=pltpu.SMEM)
    anywhere = pl.BlockSpec(memory_space=pl.ANY)
    hbm = pl.BlockSpec(memory_space=pltpu.HBM)
    return pl.pallas_call(
        functools.partial(attention_body, first, span, homes, rounds, layers),
        out_shape=jax.ShapeDtypeStruct((span, tokens, HD), jnp.bfloat16),
        in_specs=[smem, smem, smem] + [hbm] + [anywhere] * len(sources),
        out_specs=pl.BlockSpec(memory_space=pltpu.VMEM),
        scratch_shapes=[
            pltpu.VMEM((span, tokens, HD), jnp.bfloat16),
            pltpu.VMEM((span, 3, 2, tokens, HD), jnp.bfloat16),
            pltpu.VMEM((NB * CELLS, HD), jnp.bfloat16),
            pltpu.VMEM((NB * CELLS, HD), jnp.bfloat16),
            pltpu.SemaphoreType.DMA((span, rounds)),
            pltpu.SemaphoreType.DMA((span, 3 * rounds)),
        ],
        compiler_params=pltpu.CompilerParams(vmem_limit_bytes=60 * MIB),
        cost_estimate=pl.CostEstimate(flops=1, bytes_accessed=1, transcendentals=0),
    )(slots, counts, strips, queries_in, *sources)


def output_body(rounds, rows, strips, *refs):
    count = rounds * len(BATCHES) * 2
    pieces = refs[:count]
    w_own, w_got, w_also, gate, out, mixed, weight, sems, weight_sems = refs[count:]
    part = rows * TW
    steps, _, step = weight.shape
    own_half, own_clip = strips[rounds + 1], strips[rounds + 2]
    n = pl.program_id(0)

    @pl.when(n == 0)
    def _():
        copies = []
        for i in range(rounds):
            for batch, (first, span) in enumerate(BATCHES):
                for spot in range(2 * span):
                    column = 2 * first + spot
                    copy = pltpu.make_async_copy(
                        pieces[(i * len(BATCHES) + batch) * 2 + spot // span].at[spot % span],
                        mixed.at[pl.ds(i * 2 * part, 2 * part), pl.ds(column * HD, HD)],
                        sems.at[i, column],
                    )
                    copy.start()
                    copies.append(copy)
        for k in range(steps):
            in_own = (k // (steps // 2)) == own_half
            columns = pl.ds(k % (steps // 2) * step, step)
            for batch, (first, span) in enumerate(BATCHES):
                block = span * HD
                for over_blk in range(2):
                    half = own_half ^ over_blk
                    target = weight.at[k, pl.ds((2 * first + over_blk * span) * HD, block)]
                    sem = weight_sems.at[k, batch * 2 + over_blk]
                    own_row = pl.multiple_of((half * HPD + first) * HD, HD)
                    far_row = first * HD

                    @pl.when(in_own)
                    def _():
                        pltpu.make_async_copy(
                            w_own.at[pl.ds(own_row, block), columns], target, sem
                        ).start()

                    @pl.when(jnp.logical_and(jnp.logical_not(in_own), half == own_clip))
                    def _():
                        pltpu.make_async_copy(
                            w_got.at[pl.ds(far_row, block), columns], target, sem
                        ).start()

                    @pl.when(jnp.logical_and(jnp.logical_not(in_own), half != own_clip))
                    def _():
                        pltpu.make_async_copy(
                            w_also.at[pl.ds(far_row, block), columns], target, sem
                        ).start()

        for copy in copies:
            copy.wait()

    for batch, (first, span) in enumerate(BATCHES):
        for over_blk in range(2):
            pltpu.make_async_copy(
                w_own.at[pl.ds(0, span * HD), pl.ds(0, step)],
                weight.at[n, pl.ds((2 * first + over_blk * span) * HD, span * HD)],
                weight_sems.at[n, batch * 2 + over_blk],
            ).wait()
    product = jnp.dot(mixed[...], weight[n], preferred_element_type=jnp.float32) * gate[...]
    ordered = strips[rounds] == 0
    for i in range(rounds):
        strip = strips[i]
        for row in range(rows):
            base = i * 2 * part + row * TW
            near, far = product[base : base + TW], product[base + part : base + part + TW]
            both = jnp.concatenate(
                [jnp.where(ordered, near, far), jnp.where(ordered, far, near)], axis=0
            )
            out[row, strip] = both.astype(jnp.bfloat16)


def project_out(strips, pieces, weights, gate, rows):
    rounds = len(pieces) // (2 * len(BATCHES))
    depth, width = weights[0].shape[0], gate.shape[1]
    step = 512
    steps = width // step
    anywhere = pl.BlockSpec(memory_space=pl.ANY)
    return pl.pallas_call(
        lambda strips_ref, *refs: output_body(rounds, rows, strips_ref, *refs),
        out_shape=jax.ShapeDtypeStruct((rows, rounds, 2 * TW, width), jnp.bfloat16),
        grid=(steps,),
        in_specs=[pl.BlockSpec(memory_space=pltpu.SMEM)]
        + [anywhere] * (len(pieces) + 3)
        + [pl.BlockSpec((1, step), lambda n: (0, n))],
        out_specs=pl.BlockSpec((rows, rounds, 2 * TW, step), lambda n: (0, 0, 0, n)),
        scratch_shapes=[
            pltpu.VMEM((rounds * rows * 2 * TW, depth), jnp.bfloat16),
            pltpu.VMEM((steps, depth, step), jnp.bfloat16),
            pltpu.SemaphoreType.DMA((rounds, 2 * HPD)),
            pltpu.SemaphoreType.DMA((steps, 2 * len(BATCHES))),
        ],
        compiler_params=pltpu.CompilerParams(vmem_limit_bytes=60 * MIB),
    )(strips, *pieces, *weights, gate)


def local(modulated, mod_gate, w_qkv, w_out, kv_tiles, kv_count):
    tok_rows, depth = modulated.shape
    seq_count = lax.axis_size("seq")
    rounds = seq_count // 2
    rows = tok_rows // (seq_count * TW)
    part = rows * TW
    strip_tokens = rounds * 4 * part
    layers = strip_tokens // (TF * GH * TH * TW)
    seq_index = lax.axis_index("seq")
    strip, half = seq_index // 2, seq_index % 2
    blk, clip = lax.axis_index("blk"), lax.axis_index("clip")

    def swap(array, over_blk, over_clip):
        return permuted(
            array, seq_count, lambda s, h, b, c: (s, h, b ^ over_blk, c ^ over_clip)
        )

    def regroup(array, distance, flip=0):
        return permuted(array, seq_count, lambda s, h, b, c: (s ^ distance, c, b, h ^ flip))

    by_strip = modulated.reshape(rows, rounds, 2, TW, depth)
    order = jnp.stack(
        [
            (clip ^ flip) * 2 + (blk ^ over_blk)
            for flip in range(2)
            for over_blk in range(2)
        ]
    ).astype(jnp.int32)
    units = [(i, flip) for i in range(rounds) for flip in range(2)]
    near = len(units) // 2
    w_half = w_out.shape[0] // 2
    live = {"w": lax.dynamic_slice_in_dim(w_out, clip * w_half, w_half, axis=0)}
    for n, (i, flip) in enumerate(units):
        sent = lax.dynamic_index_in_dim(by_strip, strip ^ i, 1, keepdims=False)
        sent = lax.dynamic_index_in_dim(sent, half ^ flip, 1, keepdims=False)
        live["send", n] = sent.reshape(part, depth)

    def outward(s, h, b, c):
        goal = s + (1 if c else -1)
        return (goal, h, b, 1 - c) if 0 <= goal < rounds else None

    def halo(group):
        live["outer", group] = permuted(live["own", group], seq_count, outward)
        live["inner", group] = swap(live["own", group], 0, 1)

    last_step = near + 1
    when = {i: i + 2 for i in range(rounds)}
    members = [
        [i for i in range(rounds) if when[i] < near],
        [i for i in range(rounds) if when[i] == near],
        [i for i in range(rounds) if when[i] == last_step],
    ]
    homes = tuple(
        next((g, some.index(i)) for g, some in enumerate(members) if i in some)
        for i in range(rounds)
    )
    for step in range(last_step + 1):
        before = dict(live)
        fetched = [near + step] if step < near else []
        fetched += [n for n in ((0, 1, 2) if step == 0 else (2 * step + 1, 2 * step + 2)) if n < near]
        mirrored = [2 * step - 2, 2 * step - 1] if 1 <= step <= near else []
        for n in fetched:
            live["piece", n] = regroup(live.pop(("send", n)), *units[n])
        for n in mirrored:
            live["mirror", n] = swap(before["piece", n], 1, 0)
        if step == near:
            halo(0)
        if step == last_step:
            halo(1)
            w_got = swap(live.pop("w"), 1, 0)
        for i in range(rounds):
            if when[i] != step:
                continue
            quad = [live.pop((kind, 2 * i + f)) for f in range(2) for kind in ("piece", "mirror")]
            if part % 16:
                quad = [
                    jnp.take(jnp.stack(quad), jnp.argsort(order), axis=0).reshape(4 * part, depth)
                ]
            group, spot = homes[i]
            live["query"], live["own", group] = project(
                order * 0 if part % 16 else order,
                quad,
                w_qkv,
                (i, spot),
                (rounds, len(members[group])),
                live.get("query"),
                live.get(("own", group)),
            )
        if step < last_step:
            names = list(live)
            live = dict(zip(names, lax.optimization_barrier([live[name] for name in names])))
    live["own", 2] = after(live["own", 2], live["outer", 1])
    halo(2)
    query = live["query"]
    sources = [live[kind, group] for group in range(3) for kind in ("own", "outer", "inner")]

    lists = jnp.concatenate([kv_tiles, kv_count[:, None]], axis=1)
    lists = regroup(lists, 0).reshape(layers * GH, seq_count, NB + 1)
    column = strip * 2 + clip
    lists = lax.dynamic_index_in_dim(lists, column, 1, keepdims=False)
    counts = lists[:, NB]
    tiles = lists[:, :NB]
    side = tiles % seq_count - column
    from_outer = (side == 1) == (clip == 1)
    source = jnp.where(side == 0, 0, jnp.where(from_outer, 1, 2))
    slots = (source * (layers * GH) + tiles // seq_count).reshape(-1)

    outer_strip = strip + 2 * clip - 1
    spots = jnp.stack(
        [strip ^ i for i in range(rounds)]
        + [(outer_strip ^ i) & (rounds - 1) for i in range(rounds)]
        + [strip ^ i for i in range(rounds)]
    ).astype(jnp.int32)


    returned, core = {}, None
    for batch, (first, span) in enumerate(BATCHES):
        asked = after(query, core) if batch else query
        result = attend(first, span, homes, slots, counts, spots, asked, sources)
        result = result.reshape(span, rounds, 2, 2, part, HD)
        kept = lax.dynamic_index_in_dim(result, clip, 2, keepdims=False)
        given = lax.dynamic_index_in_dim(result, 1 - clip, 2, keepdims=False)
        if batch:
            early = [returned[0, i, over] for i in range(rounds // 2, rounds) for over in range(2)]
            given = after(given, *early)
        core = swap(given, 0, 1)
        if not batch:
            w_also = swap(after(w_got, core), 0, 1)
        both = jnp.stack([kept, core], axis=3)
        for i in range(rounds):
            for over in range(2):
                sent = lax.dynamic_index_in_dim(both, blk ^ over, 2, keepdims=False)
                sent = lax.dynamic_index_in_dim(sent, strip ^ i, 1, keepdims=False)
                returned[batch, i, over] = permuted(
                    sent.reshape(span, 2 * part, HD),
                    seq_count,
                    lambda s, h, b, c: (s ^ i, c, b ^ over, h),
                )

    strips = jnp.stack([strip ^ i for i in range(rounds)] + [half, blk, clip]).astype(jnp.int32)
    flat = [
        returned[batch, i, over]
        for i in range(rounds)
        for batch in range(len(BATCHES))
        for over in range(2)
    ]
    out = project_out(strips, flat, (w_out, w_got, w_also), mod_gate.reshape(1, -1), rows)
    return out.reshape(tok_rows, -1)


def solution(mesh):
    return jax.shard_map(
        local,
        mesh=mesh,
        in_specs=(
            P(("clip", "seq", "blk"), None),
            P("clip"),
            P(None, "blk"),
            P(None, "blk"),
            P("clip", None),
            P("clip"),
        ),
        out_specs=P(("clip", "seq", "blk"), None),
        check_vma=False,
    )
```

```python
import functools
import math

import jax
import jax.numpy as jnp
from jax import lax
from jax.experimental import pallas as pl
from jax.experimental.pallas import tpu as pltpu
from jax.sharding import PartitionSpec as P

HD = 128
NH = 12
TF = 6
TH = 8
TW = 8
NB = 6
GH = 2
CELLS = TF * TH * TW
AXES = ("seq", "blk", "clip")
HPD = NH // 2
PAIR = 2
BATCHES = ((0, 3), (3, 3))
EXP2_SCALE = math.log2(math.e) / math.sqrt(HD)
MIB = 1 << 20
ROW_BLOCK = 192
AHEAD = 1


def permuted(array, seq_count, target):
    pairs = []
    for seq in range(seq_count):
        for blk in range(2):
            for clip in range(2):
                goal = target(seq // 2, seq % 2, blk, clip)
                if goal is not None:
                    strip, half, blk_to, clip_to = goal
                    pairs.append(
                        ((seq * 2 + blk) * 2 + clip, ((strip * 2 + half) * 2 + blk_to) * 2 + clip_to)
                    )
    return lax.ppermute(array, AXES, pairs)


def after(array, *others):
    return lax.optimization_barrier((array,) + others)[0]


def projection_body(count, spot_out, shared, place, *refs):
    pieces, weight = refs[:count], refs[count]
    query, keyval = refs[count + 1 + shared : count + 3 + shared]
    tokens, columns, blocks, token_sem, weight_sem, out_sem = refs[count + 3 + shared :]
    piece_rows = pieces[0].shape[0]
    loads = []
    for i in range(count):
        start = pl.multiple_of(place[i] * piece_rows, piece_rows)
        loads.append(
            pltpu.make_async_copy(
                pieces[i], tokens.at[pl.ds(start, piece_rows)], token_sem.at[i]
            )
        )
    width = PAIR * 3 * HD
    streams = []
    for batch in range(HPD // PAIR):
        streams.append(
            pltpu.make_async_copy(
                weight.at[:, pl.ds(batch * width, width)], columns.at[batch], weight_sem.at[batch]
            )
        )
    for copy in loads:
        copy.start()
    for copy in streams:
        copy.start()
    for copy in loads:
        copy.wait()
    stores = []
    for batch in range(HPD // PAIR):
        streams[batch].wait()
        total = jnp.dot(tokens[...], columns[batch], preferred_element_type=jnp.float32)
        for spot in range(PAIR):
            head = batch * PAIR + spot
            for kind in range(3):
                start = (spot * 3 + kind) * HD
                blocks[head, kind] = total[:, start : start + HD].astype(jnp.bfloat16)
            for target, some in (
                (query.at[spot_out[0], head], blocks.at[head, 0]),
                (keyval.at[spot_out[1], head], blocks.at[head, pl.ds(1, 2)]),
            ):
                copy = pltpu.make_async_copy(some, target, out_sem.at[len(stores)])
                copy.start()
                stores.append(copy)
    for copy in stores:
        copy.wait()


def project(place, pieces, weight, spot_out, sizes, query, keyval):
    count = len(pieces)
    given = [array for array in (query, keyval) if array is not None]
    aliases = {}
    for array, out in ((query, 0), (keyval, 1)):
        if array is not None:
            aliases[count + 2 + len(aliases)] = out
    piece_rows, depth = pieces[0].shape
    chunk = count * piece_rows
    hbm = pl.BlockSpec(memory_space=pltpu.HBM)
    return pl.pallas_call(
        functools.partial(projection_body, count, spot_out, len(given)),
        out_shape=[
            jax.ShapeDtypeStruct((sizes[0], HPD, chunk, HD), jnp.bfloat16),
            jax.ShapeDtypeStruct((sizes[1], HPD, 2, chunk, HD), jnp.bfloat16),
        ],
        in_specs=[pl.BlockSpec(memory_space=pltpu.SMEM)] + [hbm] * (count + 1 + len(given)),
        out_specs=[hbm] * 2,
        input_output_aliases=aliases,
        scratch_shapes=[
            pltpu.VMEM((chunk, depth), jnp.bfloat16),
            pltpu.VMEM((HPD // PAIR, depth, PAIR * 3 * HD), jnp.bfloat16),
            pltpu.VMEM((HPD, 3, chunk, HD), jnp.bfloat16),
            pltpu.SemaphoreType.DMA((count,)),
            pltpu.SemaphoreType.DMA((HPD // PAIR,)),
            pltpu.SemaphoreType.DMA((2 * HPD,)),
        ],
        compiler_params=pltpu.CompilerParams(vmem_limit_bytes=60 * MIB),
        cost_estimate=pl.CostEstimate(flops=1, bytes_accessed=1, transcendentals=0),
    )(place, *pieces, weight, *given)


def attention_body(first, span, homes, rounds, layers, slots, counts, strips, *refs):
    count = 1 + 3 * (1 + max(group for group, _ in homes))
    queries_in, sources = refs[0], refs[1:count]
    out, query, keyvals, query_sems, key_sems = refs[count:]
    chunk = query.shape[1] // rounds
    copies = [[] for _ in range(span)]
    for spot in range(span):
        head = first + spot
        for i in range(rounds):
            for column in range(3):
                at = pl.ds(pl.multiple_of(strips[column * rounds + i] * chunk, chunk), chunk)
                copies[spot].append(
                    pltpu.make_async_copy(
                        sources[3 * homes[i][0] + column].at[homes[i][1], head],
                        keyvals.at[spot, column, :, at],
                        key_sems.at[spot, 3 * i + column],
                    )
                )
            at = pl.ds(pl.multiple_of(strips[i] * chunk, chunk), chunk)
            copies[spot].append(
                pltpu.make_async_copy(
                    queries_in.at[i, head], query.at[spot, at], query_sems.at[spot, i]
                )
            )
    for some in copies:
        for copy in some:
            copy.start()

    def cells(layer, half):
        return [
            pl.ds(pl.multiple_of(((layer * TF + frame) * GH + half) * TH * TW, TH * TW), TH * TW)
            for frame in range(TF)
        ]

    def one_tile(spot, tile, carry):
        layer = tile // GH
        half = tile % GH

        def with_slots(count):
            parts = ([], [])
            for slot in range(count):
                found = slots[tile * NB + slot]
                column = found // (layers * GH)
                for rows in cells(found // GH % layers, found % GH):
                    for kind in range(2):
                        parts[kind].append(keyvals[spot, column, kind, rows])
            keys, values = (jnp.concatenate(some, axis=0) for some in parts)
            queries = jnp.concatenate([query[spot, rows] for rows in cells(layer, half)], axis=0)
            results = []
            starts = list(range(0, CELLS, ROW_BLOCK))

            def scores_of(row):
                return lax.dot_general(
                    queries[row : row + ROW_BLOCK],
                    keys,
                    (((1,), (1,)), ((), ())),
                    preferred_element_type=jnp.float32,
                )

            ready = [scores_of(row) for row in starts[:AHEAD]]
            for i in range(len(starts)):
                if i + AHEAD < len(starts):
                    ready.append(scores_of(starts[i + AHEAD]))
                scores = ready[i]
                peak = jnp.max(scores, axis=1, keepdims=True)
                weights = jnp.exp2(scores * EXP2_SCALE - peak * EXP2_SCALE)
                denom = jnp.sum(weights, axis=1, keepdims=True)
                mixed = jnp.dot(
                    weights.astype(jnp.bfloat16),
                    values,
                    preferred_element_type=jnp.float32,
                )
                results.append(mixed / denom)
            result = jnp.concatenate(results, axis=0).astype(jnp.bfloat16)
            for frame, rows in enumerate(cells(layer, half)):
                out[spot, rows] = result[frame * TH * TW : (frame + 1) * TH * TW]

        for count in range(1, NB + 1):
            pl.when(counts[tile] == count)(functools.partial(with_slots, count))
        return carry

    for spot in range(span):
        for copy in copies[spot]:
            copy.wait()
        lax.fori_loop(0, layers * GH, functools.partial(one_tile, spot), 0)


def attend(first, span, homes, slots, counts, strips, queries_in, sources):
    rounds, _, chunk, _ = queries_in.shape
    tokens = rounds * chunk
    layers = tokens // (TF * GH * TH * TW)
    smem = pl.BlockSpec(memory_space=pltpu.SMEM)
    anywhere = pl.BlockSpec(memory_space=pl.ANY)
    hbm = pl.BlockSpec(memory_space=pltpu.HBM)
    return pl.pallas_call(
        functools.partial(attention_body, first, span, homes, rounds, layers),
        out_shape=jax.ShapeDtypeStruct((span, tokens, HD), jnp.bfloat16),
        in_specs=[smem, smem, smem] + [hbm] + [anywhere] * len(sources),
        out_specs=pl.BlockSpec(memory_space=pltpu.VMEM),
        scratch_shapes=[
            pltpu.VMEM((span, tokens, HD), jnp.bfloat16),
            pltpu.VMEM((span, 3, 2, tokens, HD), jnp.bfloat16),
            pltpu.SemaphoreType.DMA((span, rounds)),
            pltpu.SemaphoreType.DMA((span, 3 * rounds)),
        ],
        compiler_params=pltpu.CompilerParams(vmem_limit_bytes=60 * MIB),
        cost_estimate=pl.CostEstimate(flops=1, bytes_accessed=1, transcendentals=0),
    )(slots, counts, strips, queries_in, *sources)


def output_body(rounds, rows, strips, *refs):
    count = rounds * len(BATCHES) * 2
    pieces = refs[:count]
    w_own, w_got, w_also, gate, out, mixed, weight, sems, weight_sems = refs[count:]
    part = rows * TW
    steps, _, step = weight.shape
    own_half, own_clip = strips[rounds + 1], strips[rounds + 2]
    n = pl.program_id(0)

    @pl.when(n == 0)
    def _():
        copies = []
        for i in range(rounds):
            for batch, (first, span) in enumerate(BATCHES):
                for over in range(2):
                    piece = (i * len(BATCHES) + batch) * 2 + over
                    copy = pltpu.make_async_copy(
                        pieces[piece],
                        mixed.at[
                            pl.ds(2 * first + over * span, span),
                            pl.ds(i * 2 * part, 2 * part),
                        ],
                        sems.at[piece],
                    )
                    copy.start()
                    copies.append(copy)
        for k in range(steps):
            in_own = (k // (steps // 2)) == own_half
            columns = pl.ds(k % (steps // 2) * step, step)
            for batch, (first, span) in enumerate(BATCHES):
                block = span * HD
                for over_blk in range(2):
                    half = own_half ^ over_blk
                    target = weight.at[k, pl.ds((2 * first + over_blk * span) * HD, block)]
                    sem = weight_sems.at[k, batch * 2 + over_blk]
                    own_row = pl.multiple_of((half * HPD + first) * HD, HD)
                    far_row = first * HD

                    @pl.when(in_own)
                    def _():
                        pltpu.make_async_copy(
                            w_own.at[pl.ds(own_row, block), columns], target, sem
                        ).start()

                    @pl.when(jnp.logical_and(jnp.logical_not(in_own), half == own_clip))
                    def _():
                        pltpu.make_async_copy(
                            w_got.at[pl.ds(far_row, block), columns], target, sem
                        ).start()

                    @pl.when(jnp.logical_and(jnp.logical_not(in_own), half != own_clip))
                    def _():
                        pltpu.make_async_copy(
                            w_also.at[pl.ds(far_row, block), columns], target, sem
                        ).start()

        for copy in copies:
            copy.wait()

    for batch, (first, span) in enumerate(BATCHES):
        for over_blk in range(2):
            pltpu.make_async_copy(
                w_own.at[pl.ds(0, span * HD), pl.ds(0, step)],
                weight.at[n, pl.ds((2 * first + over_blk * span) * HD, span * HD)],
                weight_sems.at[n, batch * 2 + over_blk],
            ).wait()
    joined = jnp.concatenate([mixed[head] for head in range(2 * HPD)], axis=1)
    product = jnp.dot(joined, weight[n], preferred_element_type=jnp.float32) * gate[...]
    ordered = strips[rounds] == 0
    for i in range(rounds):
        strip = strips[i]
        for row in range(rows):
            base = i * 2 * part + row * TW
            near, far = product[base : base + TW], product[base + part : base + part + TW]
            both = jnp.concatenate(
                [jnp.where(ordered, near, far), jnp.where(ordered, far, near)], axis=0
            )
            out[row, strip] = both.astype(jnp.bfloat16)


def project_out(strips, pieces, weights, gate, rows):
    rounds = len(pieces) // (2 * len(BATCHES))
    depth, width = weights[0].shape[0], gate.shape[1]
    step = 512
    steps = width // step
    anywhere = pl.BlockSpec(memory_space=pl.ANY)
    return pl.pallas_call(
        lambda strips_ref, *refs: output_body(rounds, rows, strips_ref, *refs),
        out_shape=jax.ShapeDtypeStruct((rows, rounds, 2 * TW, width), jnp.bfloat16),
        grid=(steps,),
        in_specs=[pl.BlockSpec(memory_space=pltpu.SMEM)]
        + [anywhere] * (len(pieces) + 3)
        + [pl.BlockSpec((1, step), lambda n: (0, n))],
        out_specs=pl.BlockSpec((rows, rounds, 2 * TW, step), lambda n: (0, 0, 0, n)),
        scratch_shapes=[
            pltpu.VMEM((2 * HPD, rounds * rows * 2 * TW, HD), jnp.bfloat16),
            pltpu.VMEM((steps, depth, step), jnp.bfloat16),
            pltpu.SemaphoreType.DMA((len(pieces),)),
            pltpu.SemaphoreType.DMA((steps, 2 * len(BATCHES))),
        ],
        compiler_params=pltpu.CompilerParams(vmem_limit_bytes=60 * MIB),
    )(strips, *pieces, *weights, gate)


def local(modulated, mod_gate, w_qkv, w_out, kv_tiles, kv_count):
    tok_rows, depth = modulated.shape
    seq_count = lax.axis_size("seq")
    rounds = seq_count // 2
    rows = tok_rows // (seq_count * TW)
    part = rows * TW
    strip_tokens = rounds * 4 * part
    layers = strip_tokens // (TF * GH * TH * TW)
    seq_index = lax.axis_index("seq")
    strip, half = seq_index // 2, seq_index % 2
    blk, clip = lax.axis_index("blk"), lax.axis_index("clip")

    def swap(array, over_blk, over_clip):
        return permuted(
            array, seq_count, lambda s, h, b, c: (s, h, b ^ over_blk, c ^ over_clip)
        )

    def regroup(array, distance, flip=0):
        return permuted(array, seq_count, lambda s, h, b, c: (s ^ distance, c, b, h ^ flip))

    by_strip = modulated.reshape(rows, rounds, 2, TW, depth)
    order = jnp.stack(
        [
            (clip ^ flip) * 2 + (blk ^ over_blk)
            for flip in range(2)
            for over_blk in range(2)
        ]
    ).astype(jnp.int32)
    units = [(i, flip) for i in range(rounds) for flip in range(2)]
    near = len(units) // 2
    w_half = w_out.shape[0] // 2
    live = {"w": lax.dynamic_slice_in_dim(w_out, clip * w_half, w_half, axis=0)}
    for n, (i, flip) in enumerate(units):
        whole = by_strip if n in (0, 1, 2, near) else after(by_strip, live["send", 0])
        sent = lax.dynamic_index_in_dim(whole, strip ^ i, 1, keepdims=False)
        sent = lax.dynamic_index_in_dim(sent, half ^ flip, 1, keepdims=False)
        live["send", n] = sent.reshape(part, depth)

    def outward(s, h, b, c):
        goal = s + (1 if c else -1)
        return (goal, h, b, 1 - c) if 0 <= goal < rounds else None

    def halo(group):
        live["outer", group] = permuted(live["own", group], seq_count, outward)
        live["inner", group] = swap(live["own", group], 0, 1)

    last_step = near + 1
    when = {i: i + 2 for i in range(rounds)}
    members = [
        [i for i in range(rounds) if when[i] < near],
        [i for i in range(rounds) if when[i] == near],
        [i for i in range(rounds) if when[i] == last_step],
    ]
    homes = tuple(
        next((g, some.index(i)) for g, some in enumerate(members) if i in some)
        for i in range(rounds)
    )
    for step in range(last_step + 1):
        before = dict(live)
        fetched = [near + step] if step < near else []
        fetched += [n for n in ((0, 1, 2) if step == 0 else (2 * step + 1, 2 * step + 2)) if n < near]
        mirrored = [2 * step - 2, 2 * step - 1] if 1 <= step <= near else []
        for n in fetched:
            live["piece", n] = regroup(live.pop(("send", n)), *units[n])
        for n in mirrored:
            live["mirror", n] = swap(before["piece", n], 1, 0)
        if step == near:
            halo(0)
        if step == last_step:
            halo(1)
            w_got = swap(live.pop("w"), 1, 0)
        for i in range(rounds):
            if when[i] != step:
                continue
            quad = [live.pop((kind, 2 * i + f)) for f in range(2) for kind in ("piece", "mirror")]
            if part % 16:
                quad = [
                    jnp.take(jnp.stack(quad), jnp.argsort(order), axis=0).reshape(4 * part, depth)
                ]
            group, spot = homes[i]
            live["query"], live["own", group] = project(
                order * 0 if part % 16 else order,
                quad,
                w_qkv,
                (i, spot),
                (rounds, len(members[group])),
                live.get("query"),
                live.get(("own", group)),
            )
        if step < last_step:
            names = list(live)
            live = dict(zip(names, lax.optimization_barrier([live[name] for name in names])))
    live["own", 2] = after(live["own", 2], live["outer", 1])
    halo(2)
    query = live["query"]
    sources = [live[kind, group] for group in range(3) for kind in ("own", "outer", "inner")]

    lists = jnp.concatenate([kv_tiles, kv_count[:, None]], axis=1)
    lists = regroup(lists, 0).reshape(layers * GH, seq_count, NB + 1)
    column = strip * 2 + clip
    lists = lax.dynamic_index_in_dim(lists, column, 1, keepdims=False)
    counts = lists[:, NB]
    tiles = lists[:, :NB]
    side = tiles % seq_count - column
    from_outer = (side == 1) == (clip == 1)
    source = jnp.where(side == 0, 0, jnp.where(from_outer, 1, 2))
    slots = (source * (layers * GH) + tiles // seq_count).reshape(-1)

    outer_strip = strip + 2 * clip - 1
    spots = jnp.stack(
        [strip ^ i for i in range(rounds)]
        + [(outer_strip ^ i) & (rounds - 1) for i in range(rounds)]
        + [strip ^ i for i in range(rounds)]
    ).astype(jnp.int32)


    returned, core = {}, None
    for batch, (first, span) in enumerate(BATCHES):
        asked = after(query, core) if batch else query
        result = attend(first, span, homes, slots, counts, spots, asked, sources)
        result = result.reshape(span, rounds, 2, 2, part, HD)
        kept = lax.dynamic_index_in_dim(result, clip, 2, keepdims=False)
        given = lax.dynamic_index_in_dim(result, 1 - clip, 2, keepdims=False)
        if batch:
            early = [returned[0, i, over] for i in range(rounds // 2, rounds) for over in range(2)]
            given = after(given, *early)
        core = swap(given, 0, 1)
        if not batch:
            w_also = swap(after(w_got, core), 0, 1)
        both = jnp.stack([kept, core], axis=3)
        for i in range(rounds):
            for over in range(2):
                sent = lax.dynamic_index_in_dim(both, blk ^ over, 2, keepdims=False)
                sent = lax.dynamic_index_in_dim(sent, strip ^ i, 1, keepdims=False)
                returned[batch, i, over] = permuted(
                    sent.reshape(span, 2 * part, HD),
                    seq_count,
                    lambda s, h, b, c: (s ^ i, c, b ^ over, h),
                )

    strips = jnp.stack([strip ^ i for i in range(rounds)] + [half, blk, clip]).astype(jnp.int32)
    flat = [
        returned[batch, i, over]
        for i in range(rounds)
        for batch in range(len(BATCHES))
        for over in range(2)
    ]
    out = project_out(strips, flat, (w_out, w_got, w_also), mod_gate.reshape(1, -1), rows)
    return out.reshape(tok_rows, -1)


def solution(mesh):
    return jax.shard_map(
        local,
        mesh=mesh,
        in_specs=(
            P(("clip", "seq", "blk"), None),
            P("clip"),
            P(None, "blk"),
            P(None, "blk"),
            P("clip", None),
            P("clip"),
        ),
        out_specs=P(("clip", "seq", "blk"), None),
        check_vma=False,
    )
```
